512 devices in a mesh: leaf: 128 (over y, z, core), sub: 4 (over x).
Axes of the slice: x: 4, y: 8, z: 8, core: 2. Of those that a mesh axis runs over, the one named last changes fastest.
Arguments:
- points: bfloat16 [16, 1048576], P(None, ('leaf', 'sub')), may hold values from -6 to 6
- basis: bfloat16 [32, 1048576], P(None, ('leaf', 'sub')), may hold values from -0.75 to 0.75
- transfer: bfloat16 [31744, 1024], P(('leaf', 'sub')), may hold values from -0.75 to 0.75
- top_transfer: bfloat16 [1024, 1024], replicated, may hold values from -0.75 to 0.75
- coupling: bfloat16 [32256, 4, 1024], P(('leaf', 'sub'))
- far_index: int32 [32256, 4], P(('leaf', 'sub')), may hold values from 0 to 16383, as said below
- far_count: int32 [32256], P(('leaf', 'sub')), may hold values from 1 to 4, as said below
- top_coupling: bfloat16 [512, 4, 1024], P(('leaf', 'sub'))
- top_index: int32 [512, 4], P(('leaf', 'sub')), may hold values from 0 to 511, as said below
- top_count: int32 [512], P(('leaf', 'sub')), may hold values from 1 to 4
- near_block: bfloat16 [16384, 4, 4096], P(('leaf', 'sub')), may hold values from -0.375 to 0.375
- near_index: int32 [16384, 4], P(('leaf', 'sub')), may hold values from 0 to 16383, as said below
- near_count: int32 [16384], P(('leaf', 'sub')), may hold values from 1 to 4, as said below
Outputs:
- hessian_product: bfloat16 [16, 1048576], P(None, ('leaf', 'sub'))
The draws below stay inside these ranges and needn't reach their ends.
Inputs may be any that keep to these rules, and one draw needn't show every extreme that they name: `far_index`: for a cluster of a level with n = 32 >> l clusters a device, every partner lies within n of its own number. `far_count`: the first cluster of each level of each device subtree uses all slots. `top_index`: partners are nodes of the same depth within 3 positions of the node; row 0 is not read. `near_index`: slot 0 is the leaf itself; every partner lies within 32 leaves of it. `near_count`: the first leaf of each device uses all slots.
All inputs are finite; a program needn't handle non-finite values.
Results may differ from the reference program's by a relative error of at most 0.035.
Values may be sent and summed in bfloat16 or wider, within the bound.
No kernel may reach another device: no remote copies, remote signals or barrier semaphores. Data moves between devices by JAX's collectives and lax.ppermute only.
A program may use at most 64 MiB of HBM per device.

```python
import math
import jax
import jax.numpy as jnp
from jax import lax

BASIS_RANK = 32
LEAF = 64
VECTOR_COUNT = 16
FAR = 4
NEAR = 4
LPD = 32
ROOTS = 512
NPTS = 1048576


def level_index(position, leaf_count):
    local_depth = leaf_count.bit_length() - 1
    height = jnp.zeros_like(position)
    for counter in range(1, local_depth + 1):
        height = height + (position >= 2 * leaf_count - 2 * (leaf_count >> counter)).astype(jnp.int32)
    return height


def cluster_rows(leaf_count, subtrees):
    per_dev = 2 * leaf_count - 1
    row_ids = jnp.arange(per_dev * subtrees, dtype=jnp.int32)
    owner_id = row_ids // per_dev
    position = row_ids % per_dev
    height = level_index(position, leaf_count)
    width_now = jnp.right_shift(jnp.int32(leaf_count), height)
    member = position - (2 * leaf_count - 2 * width_now)
    return (owner_id, height, width_now, member)


def heap_depth(node_ids, subtrees):
    depth_top = subtrees.bit_length() - 1
    product_output = jnp.zeros_like(node_ids)
    for counter in range(1, depth_top):
        product_output = product_output + (node_ids >= 1 << counter).astype(jnp.int32)
    return product_output


def scaled_values(key, array_shape):
    values = jax.random.truncated_normal(key, -4.0, 4.0, array_shape, jnp.float32)
    return values


def draw_far_index(key, part):
    key = jax.random.fold_in(key, 11)
    owner_id, height, width_now, member = cluster_rows(LPD, ROOTS)
    target = owner_id * width_now + member
    offsets = jax.random.randint(key, (target.shape[0], FAR), 0, 1 << 20)
    span = width_now[:, None]
    shifted = target[:, None] + offsets % (2 * span + 1) - span
    return jnp.clip(shifted, 0, ROOTS * span - 1).astype(jnp.int32)


def draw_far_count(key, part):
    key = jax.random.fold_in(key, 12)
    owner_id, height, width_now, member = cluster_rows(LPD, ROOTS)
    counts = jax.random.randint(key, member.shape, 1, FAR + 1)
    return jnp.where(member == 0, FAR, counts).astype(jnp.int32)


def draw_top_index(key, part):
    key = jax.random.fold_in(key, 13)
    node_ids = jnp.arange(ROOTS, dtype=jnp.int32)
    depth_base = jnp.left_shift(jnp.int32(1), heap_depth(node_ids, ROOTS))[:, None]
    offsets = jax.random.randint(key, (ROOTS, FAR), 0, 7) - 3
    shifted = jnp.clip(node_ids[:, None] - depth_base + offsets, 0, depth_base - 1) + depth_base
    return jnp.where(node_ids[:, None] == 0, 0, shifted).astype(jnp.int32)


def draw_top_count(key, part):
    key = jax.random.fold_in(key, 14)
    node_ids = jnp.arange(ROOTS, dtype=jnp.int32)
    counts = jax.random.randint(key, (ROOTS,), 1, FAR + 1)
    counts = jnp.where(node_ids == 1, FAR, counts)
    return jnp.where(node_ids == 0, 1, counts).astype(jnp.int32)


def draw_near_index(key, part):
    key = jax.random.fold_in(key, 15)
    leaf_ids = jnp.arange(LPD * ROOTS, dtype=jnp.int32)
    offsets = jax.random.randint(key, (LPD * ROOTS, NEAR), 0, 2 * LPD + 1) - LPD
    shifted = jnp.clip(leaf_ids[:, None] + offsets, 0, LPD * ROOTS - 1)
    slot_ids = jnp.arange(NEAR, dtype=jnp.int32)[None, :]
    return jnp.where(slot_ids == 0, leaf_ids[:, None], shifted).astype(jnp.int32)


def draw_near_count(key, part):
    key = jax.random.fold_in(key, 16)
    leaf_ids = jnp.arange(LPD * ROOTS, dtype=jnp.int32)
    counts = jax.random.randint(key, (LPD * ROOTS,), 1, NEAR + 1)
    return jnp.where(leaf_ids % LPD == 0, NEAR, counts).astype(jnp.int32)


def draw_coupling(key, part):
    key = jax.random.fold_in(key, 17)
    owner_id, height, width_now, member = cluster_rows(LPD, ROOTS)
    factor = jnp.exp2(0.5 * height.astype(jnp.float32)) / math.sqrt(FAR * BASIS_RANK)
    values = scaled_values(key, (height.shape[0], FAR, BASIS_RANK * BASIS_RANK))
    return (values * factor[:, None, None]).astype(jnp.bfloat16)


def draw_top_coupling(key, part):
    key = jax.random.fold_in(key, 18)
    node_ids = jnp.arange(ROOTS, dtype=jnp.int32)
    local_depth = LPD.bit_length() - 1
    depth_top = ROOTS.bit_length() - 1
    height = local_depth + depth_top - heap_depth(node_ids, ROOTS)
    factor = jnp.exp2(0.5 * height.astype(jnp.float32)) / math.sqrt(FAR * BASIS_RANK)
    values = scaled_values(key, (ROOTS, FAR, BASIS_RANK * BASIS_RANK))
    return (values * factor[:, None, None]).astype(jnp.bfloat16)


def block_levels(stream_key, shape, cuts, smallest, top_value):
    def one(dim, shards_of):
        steps = jax.random.uniform(jax.random.fold_in(jax.random.fold_in(stream_key, 6), dim), (shards_of,), jnp.float32, smallest / len(cuts), top_value / len(cuts))
        return jnp.repeat(jnp.exp(steps), shape[dim] // shards_of).reshape((-1,) + (1,) * (len(shape) - dim - 1))

    loudness = one(*cuts[0])
    for cut in cuts[1:]:
        loudness = loudness * one(*cut)
    return loudness


def gaussian(stream_key, extent, scale, most, split=(), kind=jnp.bfloat16):
    gain = block_levels(stream_key, extent, split, -0.22, 0.18) if split else 1.0
    array = jax.random.normal(stream_key, extent, jnp.float32) * scale * gain
    return jnp.minimum(jnp.maximum(array, -most), most).astype(kind)


def setup_inputs(seed: int = 0) -> dict:
    key_of = jax.random.split(jax.random.key(seed), 14)
    return {
        "points": gaussian(key_of[0], (VECTOR_COUNT, NPTS), 1.0, 6.0, ((1, 512),)),
        "basis": gaussian(key_of[1], (BASIS_RANK, NPTS), LEAF ** -0.5, 0.75, ((1, 512),)),
        "transfer": gaussian(key_of[2], ((2 * LPD - 2) * ROOTS, BASIS_RANK * BASIS_RANK), (2 * BASIS_RANK) ** -0.5, 0.75, ((0, 512),)),
        "top_transfer": gaussian(key_of[3], (2 * ROOTS, BASIS_RANK * BASIS_RANK), (2 * BASIS_RANK) ** -0.5, 0.75),
        "coupling": draw_coupling(jax.random.fold_in(key_of[13], 71), 0),
        "far_index": draw_far_index(jax.random.fold_in(key_of[13], 71), 0),
        "far_count": draw_far_count(jax.random.fold_in(key_of[13], 71), 0),
        "top_coupling": draw_top_coupling(jax.random.fold_in(key_of[13], 71), 0),
        "top_index": draw_top_index(jax.random.fold_in(key_of[13], 71), 0),
        "top_count": draw_top_count(jax.random.fold_in(key_of[13], 71), 0),
        "near_block": gaussian(key_of[10], (LPD * ROOTS, NEAR, LEAF * LEAF), (NEAR * LEAF) ** -0.5, 0.375, ((0, 512),)),
        "near_index": draw_near_index(jax.random.fold_in(key_of[13], 71), 0),
        "near_count": draw_near_count(jax.random.fold_in(key_of[13], 71), 0),
    }


def reference(points, basis, transfer, top_transfer, coupling, far_index, far_count, top_coupling, top_index, top_count, near_block, near_index, near_count):
    local_depth = LPD.bit_length() - 1
    subtrees = ROOTS
    depth_top = subtrees.bit_length() - 1
    leaves_all = LPD * subtrees
    shaped_points = points.astype(jnp.float32).reshape(VECTOR_COUNT, leaves_all, LEAF)
    shaped_basis = basis.astype(jnp.float32).reshape(BASIS_RANK, leaves_all, LEAF)
    upward = [jnp.einsum('kjp,vjp->jkv', shaped_basis, shaped_points).astype(jnp.bfloat16)]
    rows_trans = transfer.reshape(subtrees, 2 * LPD - 2, BASIS_RANK, BASIS_RANK)
    rows_coup = coupling.reshape(subtrees, 2 * LPD - 1, FAR, BASIS_RANK, BASIS_RANK)
    rows_index = far_index.reshape(subtrees, 2 * LPD - 1, FAR)
    rows_count = far_count.reshape(subtrees, 2 * LPD - 1)

    def level_rows(source, height):
        width_now = LPD >> height
        offset = 2 * LPD - 2 * width_now
        sliced = source[:, offset:offset + width_now]
        return sliced.reshape((subtrees * width_now,) + source.shape[2:])

    def couple_rows(blocks, partners, counts):
        in_use = (jnp.arange(FAR, dtype=jnp.int32)[None, :] < counts[:, None]).astype(jnp.bfloat16)
        masked = partners * in_use[:, :, None, None]
        return jnp.einsum('gfkq,gfqv->gkv', blocks.astype(jnp.float32), masked.astype(jnp.float32)).astype(jnp.bfloat16)

    def descend_rows(parent_nodes, matrix_stack, added):
        twice_sized = jnp.repeat(parent_nodes, 2, axis=0).astype(jnp.float32)
        product_output = jnp.einsum('aux,axr->aur', matrix_stack.astype(jnp.float32).reshape(-1, BASIS_RANK, BASIS_RANK), twice_sized)
        return (product_output + added.astype(jnp.float32)).astype(jnp.bfloat16)
    for height in range(local_depth):
        matrix_stack = level_rows(rows_trans, height).astype(jnp.float32).reshape(-1, 2, BASIS_RANK, BASIS_RANK)
        paired = upward[height].astype(jnp.float32).reshape(-1, 2, BASIS_RANK, VECTOR_COUNT)
        upward.append(jnp.einsum('jckq,jckv->jqv', matrix_stack, paired).astype(jnp.bfloat16))
    coupled = []
    for height in range(local_depth + 1):
        partners = upward[height][level_rows(rows_index, height)]
        coupled.append(couple_rows(level_rows(rows_coup, height), partners, level_rows(rows_count, height)))
    tier_map = {depth_top: upward[local_depth]}
    for depth_now in range(depth_top - 1, -1, -1):
        lower_start = 1 << depth_now + 1
        matrix_stack = top_transfer[lower_start:2 * lower_start].astype(jnp.float32).reshape(-1, 2, BASIS_RANK, BASIS_RANK)
        paired = tier_map[depth_now + 1].astype(jnp.float32).reshape(-1, 2, BASIS_RANK, VECTOR_COUNT)
        tier_map[depth_now] = jnp.einsum('jckq,jckv->jqv', matrix_stack, paired).astype(jnp.bfloat16)
    heap_rows = jnp.concatenate([jnp.zeros((1, BASIS_RANK, VECTOR_COUNT), jnp.bfloat16)] + [tier_map[depth_now] for depth_now in range(depth_top)], axis=0)
    top_coupled = couple_rows(top_coupling.reshape(subtrees, FAR, BASIS_RANK, BASIS_RANK), heap_rows[top_index], top_count)
    carried = top_coupled[1:2]
    for depth_now in range(1, depth_top):
        lower_start = 1 << depth_now
        carried = descend_rows(carried, top_transfer[lower_start:2 * lower_start], top_coupled[lower_start:2 * lower_start])
    carried = descend_rows(carried, top_transfer[subtrees:2 * subtrees], coupled[local_depth])
    for height in range(local_depth - 1, -1, -1):
        carried = descend_rows(carried, level_rows(rows_trans, height), coupled[height])
    far_part = jnp.einsum('kjp,jkv->vjp', shaped_basis, carried.astype(jnp.float32))
    points_blocks = points.reshape(VECTOR_COUNT, leaves_all, LEAF)

    def near_terms(pieces):
        blocks, indices, counts = pieces
        in_use = (jnp.arange(NEAR, dtype=jnp.int32)[None, :] < counts[:, None]).astype(jnp.bfloat16)
        gathered = points_blocks[:, indices] * in_use[None, :, :, None]
        return jnp.einsum('tfpq,vtfq->vtp', blocks.astype(jnp.float32).reshape(LPD, NEAR, LEAF, LEAF), gathered.astype(jnp.float32))
    near_all = lax.map(near_terms, (near_block.reshape(subtrees, LPD, NEAR, LEAF * LEAF), near_index.reshape(subtrees, LPD, NEAR), near_count.reshape(subtrees, LPD)))
    near_part = jnp.transpose(near_all, (1, 0, 2, 3)).reshape(VECTOR_COUNT, leaves_all, LEAF)
    return (far_part + near_part).astype(jnp.bfloat16).reshape(VECTOR_COUNT, leaves_all * LEAF)
```

```python
import jax
import jax.numpy as jnp
import numpy as np
from jax import lax
from jax.experimental import pallas as pl
from jax.experimental.pallas import tpu as pltpu
from jax.sharding import Mesh
from jax.sharding import PartitionSpec as P

RANK = 32
LEAF = 64
VEC = 16
FAR = 4
NEAR = 4
LPD = 32
LEVELS = 6
OFFS = [2 * LPD - 2 * (LPD >> h) for h in range(LEVELS)]
ALL = ("y", "z", "core", "x")
PLANE = ("z", "core", "x")
REACH = 3
TAPS = 2 * REACH + 1
MSG = 160
SIZES = [(1 << d) + 2 * REACH for d in range(6)] + [8 + 6, 16 + 6, 32 + 6]
STARTS = [sum(SIZES[:d]) for d in range(9)]
NODES = sum(SIZES)
F32 = jnp.float32
BF16 = jnp.bfloat16

_l = np.arange(128)
_c = np.arange(1024)
SPREAD = (_l[:, None] == _c[None, :] // 32).astype(np.float32)
FOLD = (_l[:, None] % 32 == _l[None, :] % 32).astype(np.float32)
GATHER = (_c[:, None] // 32 == _l[None, :] % 32).astype(np.float32)
PICK = np.concatenate(
    [FOLD * (_l[:, None] // 32 == q) for q in range(4)], axis=1
)
HALF = np.concatenate(
    [
        ((_l[:, None] // 64 == h) & (_l[:, None] % 64 == _l[None, :] % 64)).astype(np.float32)
        for h in range(2)
    ],
    axis=1,
)
_p = np.arange(4096)
NEARSUM = (_p[:, None] // 64 == np.arange(256)[None, :] % 64).astype(np.float32)


def const(a):
    return jnp.asarray(a, BF16)


def dot(a, b):
    return jnp.dot(a, b, preferred_element_type=F32)


def lanes(shape, width):
    return lax.broadcasted_iota(jnp.int32, shape, len(shape) - 1) // width


def up_level(c, e, spread, fold, n):
    x = dot(c, spread)
    out = []
    for p in range(n // 2):
        t = x[32 * p : 32 * p + 16] * e[2 * p : 2 * p + 1]
        t = t + x[32 * p + 16 : 32 * p + 32] * e[2 * p + 1 : 2 * p + 2]
        q = t[:, 0:128]
        for m in range(1, 8):
            q = q + t[:, 128 * m : 128 * m + 128]
        out.append(q)
    q = jnp.concatenate(out, 0) if len(out) > 1 else out[0]
    return dot(q.astype(BF16), fold).astype(BF16)


def pack(c):
    m = c.shape[0] // 32
    c = c.reshape(m, 4, 8, 128)
    g = lanes((m, 8, 128), 32)
    r = jnp.where(
        g == 0, c[:, 0], jnp.where(g == 1, c[:, 1], jnp.where(g == 2, c[:, 2], c[:, 3]))
    )
    return r.reshape(m * 8, 128)


def unpack(r, pick):
    m = r.shape[0] // 8
    w = dot(r, pick)
    parts = [w[:, 128 * q : 128 * q + 128].reshape(m, 1, 8, 128) for q in range(4)]
    return jnp.concatenate(parts, 1).reshape(m * 32, 128)


def block_basis(basis, i):
    b = basis[:, 256 * i : 256 * i + 256]
    b = jnp.concatenate([b] * 4, 0)
    rows = lax.broadcasted_iota(jnp.int32, (128, 256), 0) // 32
    return jnp.where(rows == lanes((128, 256), 64), b, jnp.zeros_like(b))


def up_kernel(points, basis, transfer, spread, fold, root_out, stack_out, ex_out):
    pts = points[...]
    bas = basis[...].astype(F32)
    e = transfer[...].astype(F32)
    rows = []
    g = lanes((16, 128), 32)
    for i in range(8):
        bd = block_basis(bas, i).astype(BF16)
        c = lax.dot_general(
            pts[:, 256 * i : 256 * i + 256],
            bd,
            (((1,), (1,)), ((), ())),
            preferred_element_type=F32,
        )
        for k in range(4):
            rows.append(jnp.where(g == k, c, 0.0))
    c = dot(jnp.concatenate(rows, 0).astype(BF16), fold[...]).astype(BF16)
    levels = [c]
    for h in range(LEVELS - 1):
        n = LPD >> h
        c = up_level(c, e[OFFS[h] : OFFS[h] + n], spread[...], fold[...], n)
        levels.append(c)
    root = c.astype(F32)
    g8 = lanes((8, 128), 32)
    msg = jnp.where(g8 == 0, root[0:8], jnp.where(g8 == 1, root[8:16], 0.0))
    msg = jnp.concatenate([msg, msg], 0).astype(BF16)
    for i in range(32):
        root_out[16 * i : 16 * i + 16] = msg
    stack = jnp.concatenate(levels + [jnp.zeros((16, 128), BF16)], 0)
    stack_out[...] = stack
    ex_out[0:256] = pack(stack.astype(F32)).astype(BF16)
    for i in range(16):
        ex_out[256 + 16 * i : 272 + 16 * i] = pts[:, 128 * i : 128 * i + 128]


def plane_kernel(slots, arrived, rows, tops, spread, fold, pick, msg_out, own_out):
    w = dot(arrived[...], pick[:, 0:256])
    c = jnp.concatenate(
        [w[:, 0:128].reshape(64, 1, 8, 128), w[:, 128:256].reshape(64, 1, 8, 128)], 1
    )
    c = c.reshape(1024, 128).astype(BF16)
    e = rows[...].astype(F32)
    levels = []
    at = 0
    n = 64
    while n > 1:
        c = up_level(c, e[at : at + n], spread[...], fold[...], n)
        levels.append(c)
        at += n
        n //= 2
    d8, d7, d6, d5, d4, d3 = levels
    own_out[0:128] = d6
    own_out[128:384] = d7
    own_out[384:896] = d8
    last = [d6[80:128], d7[208:256], d8[464:512]]
    nodes = [d3, d4, d5, d6[0:48], d7[0:48], d8[0:48]] + last + [jnp.zeros((16, 128), BF16)]
    packed = pack(jnp.concatenate(nodes, 0).astype(F32))
    b = tops[...].astype(F32)
    taps = []
    for o in range(TAPS):
        t = jnp.zeros((8, 128), F32)
        for f in range(FAR):
            t = t + jnp.where(slots[f] == o, b[8 * f : 8 * f + 8], 0.0)
        taps.append(t)
    msg = jnp.concatenate(taps + [packed], 0).astype(BF16)
    for p in range(8):
        msg_out[MSG * p : MSG * p + MSG] = msg


def top_kernel(at, arrived, own, rows, spread, fold, pick, gather, out, table):
    table[...] = jnp.zeros((NODES * 16, 128), F32)

    def put(depth, place, value):
        s = (STARTS[depth] + place) * 16
        table[s : s + value.shape[0]] = value

    d3 = []
    for p in range(8):
        c = unpack(arrived[MSG * p + 48 : MSG * p + 96][8:40], pick[...])
        d3.append(c[0:16])
        put(4, REACH + 2 * p, c[16:48])
        put(5, REACH + 4 * p, c[48:112])
    c = jnp.concatenate(d3, 0)
    put(3, REACH, c)
    c = c.astype(BF16)
    e = rows[...].astype(F32)
    c = up_level(c, e[0:8], spread[...], fold[...], 8)
    put(2, REACH, c.astype(F32))
    c = up_level(c, e[8:12], spread[...], fold[...], 4)
    put(1, REACH, c.astype(F32))
    c = up_level(c, e[12:14], spread[...], fold[...], 2)
    put(0, REACH, c.astype(F32))
    prior = unpack(arrived[pl.ds(pl.multiple_of(at[0] * MSG, 16), MSG)][80:160], pick[...])
    later = unpack(arrived[pl.ds(pl.multiple_of(at[1] * MSG, 16), MSG)][80:160], pick[...])
    mine = own[...].astype(F32)
    for i, n in enumerate((8, 16, 32)):
        put(6 + i, REACH + n, later[16 * (1 + 3 * i) : 16 * (4 + 3 * i)])
        put(6 + i, 0, prior[16 * (10 + 3 * i) : 16 * (13 + 3 * i)])
        begin = 16 * (n - 8)
        put(6 + i, REACH, mine[begin : begin + 16 * n])
    sums = []
    for s in range(4):
        taps = arrived[pl.ds(pl.multiple_of(at[2 + s] * MSG, 16), MSG)][0:64].astype(F32)
        acc = [None] * 8
        for o in range(TAPS):
            c = table[pl.ds(pl.multiple_of((at[6 + s] + o) * 16, 16), 16)]
            for m in range(8):
                t = taps[8 * o + m : 8 * o + m + 1] * c
                acc[m] = t if o == 0 else acc[m] + t
        sums.append(jnp.concatenate(acc, 1))
    z = dot(jnp.concatenate(sums, 0).astype(BF16), gather[...])
    z = pack(z).astype(BF16)
    for i in range(64):
        out[16 * i : 16 * i + 16] = z


def couple_kernel(idx, before, stack, after, coupling, pick, gather, out, table, prod):
    table[0:1024] = unpack(before[0:256], pick[...])
    table[1024:2048] = stack[...].astype(F32)
    table[2048:3072] = unpack(after[0:256], pick[...])
    prod[1008:1024] = jnp.zeros((16, 1024), BF16)

    @pl.loop(0, 63, unroll=3)
    def _(t):
        b = coupling[t].astype(F32)
        acc = [None] * 8
        for f in range(FAR):
            c = table[pl.ds(pl.multiple_of(idx[t, f], 16), 16)]
            for m in range(8):
                r = b[f : f + 1, 128 * m : 128 * m + 128] * c
                acc[m] = r if f == 0 else acc[m] + r
        prod[pl.ds(pl.multiple_of(t * 16, 16), 16)] = jnp.concatenate(acc, 1).astype(BF16)

    out[...] = dot(prod[...], gather[...]).astype(BF16)


def near_kernel(idx, before, points, after, block, half, nearsum, out, table, prod):
    window = [before[256:512]]
    window += [points[:, 128 * i : 128 * i + 128] for i in range(16)]
    window += [after[256:512]]
    w = dot(jnp.concatenate(window, 0), half[...])
    w = jnp.concatenate(
        [w[:, 0:128].reshape(48, 1, 16, 128), w[:, 128:256].reshape(48, 1, 16, 128)], 1
    )
    table[0:1536] = w.reshape(1536, 128)
    table[1536:1552] = jnp.zeros((16, 128), F32)

    @pl.loop(0, LPD)
    def _(t):
        b = block[t].astype(F32)
        c = [table[pl.ds(pl.multiple_of(idx[t, f], 16), 16)] for f in range(NEAR)]
        acc = []
        for m in range(32):
            s = slice(128 * m, 128 * m + 128)
            r = b[0:1, s] * c[0]
            for f in range(1, NEAR):
                r = r + b[f : f + 1, s] * c[f]
            acc.append(r.astype(BF16))
        prod[pl.ds(pl.multiple_of(t * 16, 16), 16)] = jnp.concatenate(acc, 1)

    r = dot(prod[...], nearsum[...])
    g = lanes((16, 256), 64)
    for i in range(8):
        t = r[64 * i : 64 * i + 16]
        for k in range(1, 4):
            t = jnp.where(g == k, r[64 * i + 16 * k : 64 * i + 16 * k + 16], t)
        out[:, 256 * i : 256 * i + 256] = t


def down_kernel(at, arrived, rows, zl, transfer, basis, near, pick, gather, out):
    got = [arrived[pl.ds(pl.multiple_of(at[d] * 16, 16), 16)] for d in range(9)]
    first = [unpack(got[d][0:8], pick[...]) for d in range(7)]
    second = [unpack(got[d][8:16], pick[...]) for d in (7, 8)]
    z = [first[d][0:16] for d in range(6)]
    z += [first[6][16:32], second[0][0:16], second[1][16:32]]
    zloc = zl[...].astype(F32)
    z.append(zloc[992:1008])
    e = rows[...].astype(F32)

    def spread_down(y, row):
        return jnp.concatenate([y * row[:, 128 * m : 128 * m + 128] for m in range(8)], 1)

    y = z[0]
    for d in range(1, 10):
        t = spread_down(y, e[d - 1 : d]).astype(BF16)
        y = (dot(t, gather[...]) + z[d]).astype(BF16).astype(F32)
    e = transfer[...].astype(F32)
    for h in range(LEVELS - 2, -1, -1):
        n = LPD >> h
        t = [
            spread_down(y[16 * (j // 2) : 16 * (j // 2) + 16], e[OFFS[h] + j : OFFS[h] + j + 1])
            for j in range(n)
        ]
        t = jnp.concatenate(t, 0).astype(BF16)
        zs = zloc[16 * OFFS[h] : 16 * (OFFS[h] + n)]
        y = (dot(t, gather[...]) + zs).astype(BF16).astype(F32)
    bas = basis[...].astype(F32)
    g = lanes((16, 128), 32)
    for i in range(8):
        t = y[64 * i : 64 * i + 16]
        for k in range(1, 4):
            t = jnp.where(g == k, y[64 * i + 16 * k : 64 * i + 16 * k + 16], t)
        s = slice(256 * i, 256 * i + 256)
        far = dot(t.astype(BF16), block_basis(bas, i).astype(BF16))
        out[:, s] = (far + near[:, s]).astype(BF16)


def call(kernel, out, scratch, n_smem, args, flops, moved):
    specs = [pl.BlockSpec(memory_space=pltpu.SMEM)] * n_smem
    specs += [pl.BlockSpec(memory_space=pltpu.VMEM)] * (len(args) - n_smem)
    outs = jax.tree.map(lambda s: pl.BlockSpec(memory_space=pltpu.VMEM), out)
    return pl.pallas_call(
        kernel,
        out_shape=out,
        in_specs=specs,
        out_specs=outs,
        scratch_shapes=scratch,
        compiler_params=pltpu.CompilerParams(vmem_limit_bytes=48 << 20),
        cost_estimate=pl.CostEstimate(flops=flops, bytes_accessed=moved, transcendentals=0),
    )(*args)


def shape(rows, cols, dtype=BF16):
    return jax.ShapeDtypeStruct((rows, cols), dtype)


def local(
    points,
    basis,
    transfer,
    top_transfer,
    coupling,
    far_index,
    far_count,
    top_coupling,
    top_index,
    top_count,
    near_block,
    near_index,
    near_count,
):
    y = lax.axis_index("y")
    device = lax.axis_index(ALL)
    low = device % 64
    spread, fold, gather, pick = const(SPREAD), const(FOLD), const(GATHER), const(PICK)
    half, nearsum = const(HALF), const(NEARSUM)

    root_msg, stack, ex = call(
        up_kernel,
        (shape(512, 128), shape(1024, 128), shape(512, 128)),
        [],
        0,
        (points, basis, transfer, spread, fold),
        200_000_000,
        2_000_000,
    )
    plane_roots = lax.all_to_all(root_msg, PLANE, 0, 0, tiled=True)
    devices = 512
    before = lax.ppermute(ex, ALL, [(i, i + 1) for i in range(devices - 1)])
    after = lax.ppermute(ex, ALL, [(i + 1, i) for i in range(devices - 1)])

    ids = [(n << 3) + y * n + jnp.arange(n) for n in (64, 32, 16, 8, 4, 2)]
    ids += [jnp.arange(8, 16), jnp.arange(4, 8), jnp.arange(2, 4)]
    ids += [jnp.right_shift(devices + device, 9 - jnp.arange(1, 10)), jnp.zeros((3,), jnp.int32)]
    top_rows = top_transfer[jnp.concatenate([i.astype(jnp.int32) for i in ids])]

    tap = top_index[0] - device + REACH
    live = (jnp.arange(FAR, dtype=jnp.int32) < top_count[0]) & (device > 0)
    tap = jnp.where(live, tap, -1)
    msg, own = call(
        plane_kernel,
        (shape(8 * MSG, 128), shape(896, 128)),
        [],
        1,
        (
            tap,
            plane_roots,
            top_rows[0:126],
            top_coupling.reshape(32, 128),
            spread,
            fold,
            pick,
        ),
        300_000_000,
        2_000_000,
    )
    planes = lax.all_to_all(msg, "y", 0, 0, tiled=True)

    slot_plane = jnp.stack([0 * y, 0 * y + 1, 2 + y // 4, 4 + y // 2])
    depth = sum((low >= (1 << d)).astype(jnp.int32) for d in range(1, 6))
    starts = jnp.asarray(np.array(STARTS[:6], np.int32))
    place = jnp.stack(
        [
            starts[depth] + jnp.where(low > 0, low - jnp.left_shift(1, depth), 0),
            STARTS[6] + low % 8,
            STARTS[7] + low % 16,
            STARTS[8] + low % 32,
        ]
    )
    at = jnp.concatenate(
        [jnp.stack([jnp.maximum(y - 1, 0), jnp.minimum(y + 1, 7)]), slot_plane, place]
    ).astype(jnp.int32)
    z_msg = call(
        top_kernel,
        shape(1024, 128),
        [pltpu.VMEM((NODES * 16, 128), F32)],
        1,
        (at, planes, own, top_rows[126:140], spread, fold, pick, gather),
        200_000_000,
        2_000_000,
    )
    z_all = lax.all_to_all(z_msg, PLANE, 0, 0, tiled=True)

    where_near = near_index - (device - 1) * LPD
    used = jnp.arange(NEAR, dtype=jnp.int32)[None, :] < near_count[:, None]
    near_at = jnp.where(used, where_near, 3 * LPD) * 16
    near = call(
        near_kernel,
        shape(VEC, LPD * LEAF, F32),
        [pltpu.VMEM((1552, 128), F32), pltpu.VMEM((512, 4096), BF16)],
        1,
        (near_at, before, points, after, near_block, half, nearsum),
        2_000_000_000,
        8_000_000,
    )

    width = np.concatenate([np.full(LPD >> h, LPD >> h) for h in range(LEVELS)])
    offset = np.concatenate([np.full(LPD >> h, OFFS[h]) for h in range(LEVELS)])
    width = jnp.asarray(width[:, None].astype(np.int32))
    offset = jnp.asarray(offset[:, None].astype(np.int32))
    inside = far_index - (device - 1) * width
    used = jnp.arange(FAR, dtype=jnp.int32)[None, :] < far_count[:, None]
    which = (inside >= width).astype(jnp.int32) + (inside >= 2 * width).astype(jnp.int32)
    far_at = jnp.where(used, which * 64 + offset + inside - which * width, 63 + 64) * 16
    zl = call(
        couple_kernel,
        shape(1024, 128),
        [pltpu.VMEM((3072, 128), F32), pltpu.VMEM((1024, 1024), BF16)],
        1,
        (far_at, before, stack, after, coupling, pick, gather),
        1_000_000_000,
        6_000_000,
    )

    source = jnp.right_shift(devices + device, 9 - jnp.arange(9)).astype(jnp.int32) % 64
    return call(
        down_kernel,
        shape(VEC, LPD * LEAF),
        [],
        1,
        (source, z_all, top_rows[140:149], zl, transfer, basis, near, pick, gather),
        300_000_000,
        2_000_000,
    )


def solution(mesh):
    grid = Mesh(mesh.devices.reshape(8, 8, 2, 4), ALL)
    one, two, three = P(ALL), P(ALL, None), P(ALL, None, None)
    wide = P(None, ALL)
    placed = (wide, wide, two, P(), three, two, one, three, two, one, three, two, one)
    return jax.shard_map(local, mesh=grid, in_specs=placed, out_specs=wide, check_vma=False)
```

```python
import jax
import jax.numpy as jnp
import numpy as np
from jax import lax
from jax.experimental import pallas as pl
from jax.experimental.pallas import tpu as pltpu
from jax.sharding import Mesh
from jax.sharding import PartitionSpec as P

RANK = 32
LEAF = 64
VEC = 16
FAR = 4
NEAR = 4
LPD = 32
LEVELS = 6
OFFS = [2 * LPD - 2 * (LPD >> h) for h in range(LEVELS)]
ALL = ("y", "z", "core", "x")
PLANE = ("z", "core", "x")
REACH = 3
TAPS = 2 * REACH + 1
MSG = 176
SIZES = [(1 << d) + 2 * REACH for d in range(6)] + [8 + 6, 16 + 6, 32 + 6]
STARTS = [sum(SIZES[:d]) for d in range(9)]
NODES = sum(SIZES)
VMEM_LIMIT = 56 << 20
COST = (4, 1, 4, 3, 8, 4, 4)
F32 = jnp.float32
BF16 = jnp.bfloat16

_l = np.arange(128)
def dot(a, b):
    return jnp.dot(a, b, preferred_element_type=F32)


def lanes(shape, width):
    return lax.broadcasted_iota(jnp.int32, shape, len(shape) - 1) // width


def up_level(c, e, spread, n):
    x = dot(c, spread)
    out = []
    row = (lambda i: e[i]) if isinstance(e, list) else (lambda i: e[i : i + 1])
    for p in range(n // 2):
        t = x[32 * p : 32 * p + 16] * row(2 * p)
        t = t + x[32 * p + 16 : 32 * p + 32] * row(2 * p + 1)
        q = t[:, 0:128]
        for m in range(1, 8):
            q = q + t[:, 128 * m : 128 * m + 128]
        out.append(q)
    q = jnp.concatenate(out, 0) if len(out) > 1 else out[0]
    return q.astype(BF16)


def up_levels(c, rows):
    first, rest, fold = spread_matrix(False), spread_matrix(True), fold_matrix()
    levels = []
    n = c.shape[0] // 16
    for i, e in enumerate(rows):
        c = up_level(c, e, first if i == 0 else rest, n)
        levels.append(dot(c, fold).astype(BF16))
        n //= 2
    return levels


def pack(c):
    m = c.shape[0] // 32
    c = c.reshape(m, 4, 8, 128)
    g = lanes((m, 8, 128), 32)
    r = jnp.where(
        g == 0, c[:, 0], jnp.where(g == 1, c[:, 1], jnp.where(g == 2, c[:, 2], c[:, 3]))
    )
    return r.reshape(m * 8, 128)


def unpack(r, pick):
    m = r.shape[0] // 8
    w = dot(r, pick)
    parts = [w[:, 128 * q : 128 * q + 128].reshape(m, 1, 8, 128) for q in range(4)]
    return jnp.concatenate(parts, 1).reshape(m * 32, 128)


def block_basis(basis, i):
    b = basis[:, 256 * i : 256 * i + 256]
    b = jnp.concatenate([b] * 4, 0)
    rows = lax.broadcasted_iota(jnp.int32, (128, 256), 0) // 32
    return jnp.where(rows == lanes((128, 256), 64), b, jnp.zeros_like(b))


def iota(shape, axis, width):
    return lax.broadcasted_iota(jnp.int32, shape, axis) // width


def mask(cond):
    return jnp.where(cond, 1.0, 0.0).astype(BF16)


def spread_matrix(parts):
    r = iota((128, 1024), 0, 1)
    return mask(iota((128, 1024), 1, 32) == (r % 32 if parts else r))


def fold_matrix():
    return mask((iota((128, 128), 1, 1) - iota((128, 128), 0, 1)) % 32 == 0)


def gather_matrix():
    return mask((iota((1024, 128), 0, 32) - iota((1024, 128), 1, 1)) % 32 == 0)


def pick_matrix():
    r, c = iota((128, 512), 0, 1), iota((128, 512), 1, 1)
    return mask(((r - c) % 32 == 0) & (r // 32 == c // 128))


def pair_matrix():
    r, c = iota((256, 128), 0, 1), iota((256, 128), 1, 1)
    return mask(r % 128 // 4 * 2 + r // 128 == c % 64)


def position():
    low = (lax.axis_index("z") * 2 + lax.axis_index("core")) * 4 + lax.axis_index("x")
    return lax.axis_index("y"), low


def up_kernel(ready, points, basis, transfer, root_out, stack_out):
    fold = fold_matrix()
    ready()
    pts = points[...]
    bas = basis[...].astype(F32)
    e = transfer[...].astype(F32)
    rows = []
    g = lanes((16, 128), 32)
    for i in range(8):
        bd = block_basis(bas, i).astype(BF16)
        c = lax.dot_general(
            pts[:, 256 * i : 256 * i + 256],
            bd,
            (((1,), (1,)), ((), ())),
            preferred_element_type=F32,
        )
        for k in range(4):
            rows.append(jnp.where(g == k, c, 0.0))
    c = dot(jnp.concatenate(rows, 0).astype(BF16), fold).astype(BF16)
    below = [e[OFFS[h] : OFFS[h] + (LPD >> h)] for h in range(LEVELS - 1)]
    levels = [c] + up_levels(c, below)
    root = levels[-1].astype(F32)
    g8 = lanes((8, 128), 32)
    msg = jnp.where(g8 == 0, root[0:8], jnp.where(g8 == 1, root[8:16], 0.0))
    msg = jnp.concatenate([msg, msg], 0).astype(BF16)
    for i in range(32):
        root_out[16 * i : 16 * i + 16] = msg
    stack_out[...] = jnp.concatenate(levels + [jnp.zeros((16, 128), BF16)], 0)


def exchange_kernel(ready, stack, points, ex_out):
    ready()
    ex_out[0:256] = pack(stack[...].astype(F32)).astype(BF16)
    for i in range(16):
        ex_out[256 + 16 * i : 272 + 16 * i] = points[:, 128 * i : 128 * i + 128]


def plane_kernel(ready, index, count, arrived, rows, tops, msg_out, own_out, low_rows):
    pick = pick_matrix()
    y, low = position()
    node = y * 64 + low
    ready()
    w = dot(arrived[...], pick[:, 0:256])
    c = jnp.concatenate(
        [w[:, 0:128].reshape(64, 1, 8, 128), w[:, 128:256].reshape(64, 1, 8, 128)], 1
    )
    c = c.reshape(1024, 128).astype(BF16)
    low_rows[...] = rows[0][...].astype(F32)
    e = [rows[3][...].astype(F32), rows[2][...].astype(F32), rows[1][...].astype(F32)]
    e.append(low_rows[pl.ds(pl.multiple_of(64 + 8 * y, 8), 8)])
    for n in (4, 2):
        e.append([low_rows[pl.ds(8 * n + n * y + i, 1)] for i in range(n)])
    levels = up_levels(c, e)
    d8, d7, d6, d5, d4, d3 = levels
    own_out[0:128] = d6
    own_out[128:384] = d7
    own_out[384:896] = d8
    last = [d6[80:128], d7[208:256], d8[464:512]]
    nodes = [d3, d4, d5, d6[0:48], d7[0:48], d8[0:48]] + last + [jnp.zeros((16, 128), BF16)]
    packed = pack(jnp.concatenate(nodes, 0).astype(F32))
    b = tops[0].astype(F32)
    taps = jnp.zeros((8, 1024), F32)
    for f in range(FAR):
        tap = index[0, f] - node + REACH
        tap = jnp.where((f < count[0]) & (node > 0), tap, -1)
        taps = taps + jnp.where(iota((8, 1024), 0, 1) == tap, b[f : f + 1], 0.0)
    taps = [taps[:, 128 * m : 128 * m + 128] for m in range(8)]
    msg = jnp.concatenate(taps + [packed, jnp.zeros((8, 128), F32)], 0).astype(BF16)
    for p in range(8):
        msg_out[MSG * p : MSG * p + MSG] = msg


def top_kernel(ready, arrived, own, rows, out, table):
    pick, gather = pick_matrix(), gather_matrix()
    y, low = position()
    depth = sum((low >= (1 << d)).astype(jnp.int32) for d in range(1, 6))
    start, first = jnp.int32(STARTS[0]), jnp.int32(0)
    for d in range(6):
        start = jnp.where(depth == d, STARTS[d], start)
        first = jnp.where((depth == d) & (low > 0), 1 << d, first)
    planes = (0, 1, 2 + y // 4, 4 + y // 2)
    places = (start + low - first, STARTS[6] + low % 8, STARTS[7] + low % 16, STARTS[8] + low % 32)
    table[...] = jnp.zeros((NODES * 16, 128), F32)
    ready()

    def put(depth, place, value):
        s = (STARTS[depth] + place) * 16
        table[s : s + value.shape[0]] = value

    d3 = []
    for p in range(8):
        c = unpack(arrived[MSG * p + 64 : MSG * p + 96], pick)
        d3.append(c[0:16])
        put(4, REACH + 2 * p, c[16:48])
        put(5, REACH + 4 * p, c[48:112])
    c = jnp.concatenate(d3, 0)
    put(3, REACH, c)
    c = c.astype(BF16)
    e = rows[0][...].astype(F32)
    for d, c in zip((2, 1, 0), up_levels(c, [e[8:16], e[4:8], e[2:4]])):
        put(d, REACH, c.astype(F32))
    prior = unpack(arrived[pl.ds(pl.multiple_of(jnp.maximum(y - 1, 0) * MSG, 16), MSG)][88:168], pick)
    later = unpack(arrived[pl.ds(pl.multiple_of(jnp.minimum(y + 1, 7) * MSG, 16), MSG)][88:168], pick)
    mine = own[...].astype(F32)
    for i, n in enumerate((8, 16, 32)):
        put(6 + i, REACH + n, later[16 * (1 + 3 * i) : 16 * (4 + 3 * i)])
        put(6 + i, 0, prior[16 * (10 + 3 * i) : 16 * (13 + 3 * i)])
        begin = 16 * (n - 8)
        put(6 + i, REACH, mine[begin : begin + 16 * n])
    sums = []
    for s in range(4):
        taps = arrived[pl.ds(pl.multiple_of(planes[s] * MSG, 16), MSG)][0:64].astype(F32)
        acc = [None] * 8
        for o in range(TAPS):
            c = table[pl.ds(pl.multiple_of((places[s] + o) * 16, 16), 16)]
            for m in range(8):
                t = taps[8 * m + o : 8 * m + o + 1] * c
                acc[m] = t if o == 0 else acc[m] + t
        sums.append(jnp.concatenate(acc, 1))
    z = dot(jnp.concatenate(sums, 0).astype(BF16), gather)
    z = pack(z).astype(BF16)
    for i in range(64):
        out[16 * i : 16 * i + 16] = z


def side_kernel(
    ready,
    far_index,
    far_count,
    near_index,
    near_count,
    before,
    stack,
    after,
    points,
    coupling,
    block,
    zl_out,
    near_out,
    table,
    prod,
    leaves,
    halves,
):
    pick, gather, pair = pick_matrix(), gather_matrix(), pair_matrix()
    y, low = position()
    prior = y * 64 + low - 1
    prod[1008:1024] = jnp.zeros((16, 1024), BF16)
    ready()

    window = [before[256:512]]
    window += [points[:, 128 * i : 128 * i + 128] for i in range(16)]
    window += [after[256:512]]
    w = jnp.concatenate(window, 0).astype(F32)
    turned = jnp.concatenate([w[:, 64:128], w[:, 0:64]], 1)
    left = lanes((768, 128), 64) == 0
    four = [
        jnp.where(left, w, 0.0),
        jnp.where(left, 0.0, turned),
        jnp.where(left, turned, 0.0),
        jnp.where(left, 0.0, w),
    ]
    four = jnp.concatenate([x.reshape(48, 1, 16, 128) for x in four], 1)
    leaves[0:3072] = four.reshape(3072, 128).astype(BF16)
    leaves[3072:3104] = jnp.zeros((32, 128), BF16)
    slot = lanes((32, 128), 1) % NEAR

    def leaf(t):
        b = block[t].astype(F32)
        mat = jnp.concatenate([b[:, 128 * m : 128 * m + 128] for m in range(32)], 0)
        vec = []
        for f in range(NEAR):
            at = near_index[t, f] - prior * LPD
            at = jnp.where(f < near_count[t], at, 3 * LPD) * 32
            vec.append(leaves[pl.ds(pl.multiple_of(at, 32), 32)])
        r = lax.dot_general(
            jnp.concatenate(vec, 0),
            mat.astype(BF16),
            (((1,), (1,)), ((), ())),
            preferred_element_type=F32,
        )
        q = jnp.where(slot == 0, r[0:32], 0.0)
        for f in range(1, NEAR):
            q = jnp.where(slot == f, r[32 * f : 32 * f + 32], q)
        q = q.astype(BF16)
        at = pl.ds(pl.multiple_of(t * 16, 16), 16)
        halves[at, 0:128] = q[0:16]
        halves[at, 128:256] = q[16:32]

    pl.loop(0, LPD, unroll=4)(leaf)
    r = dot(halves[...], pair)
    g = lanes((16, 128), 64)
    for i in range(16):
        near_out[:, 128 * i : 128 * i + 128] = jnp.where(
            g == 0, r[32 * i : 32 * i + 16], r[32 * i + 16 : 32 * i + 32]
        )

    table[0:1024] = unpack(before[0:256], pick)
    table[1024:2048] = stack[...].astype(F32)
    table[2048:3072] = unpack(after[0:256], pick)

    def level(h):
        n = LPD >> h

        def step(t):
            b = coupling[t].astype(F32)
            acc = [None] * 8
            for f in range(FAR):
                at = far_index[t, f] - prior * n
                at = at + OFFS[h] + (64 - n) * (
                    (at >= n).astype(jnp.int32) + (at >= 2 * n).astype(jnp.int32)
                )
                at = jnp.where(f < far_count[t], at, 127) * 16
                c = table[pl.ds(pl.multiple_of(at, 16), 16)]
                for m in range(8):
                    r = b[f : f + 1, 128 * m : 128 * m + 128] * c
                    acc[m] = r if f == 0 else acc[m] + r
            prod[pl.ds(pl.multiple_of(t * 16, 16), 16)] = jnp.concatenate(acc, 1).astype(BF16)

        pl.loop(OFFS[h], OFFS[h] + n, unroll=min(n, 4))(step)

    for h in range(LEVELS):
        level(h)
    zl_out[...] = dot(prod[...], gather).astype(BF16)


def down_kernel(ready, arrived, rows, zl, transfer, basis, near, out, low_rows):
    pick, gather = pick_matrix(), gather_matrix()
    y, low = position()
    node = 512 + y * 64 + low
    ready()
    got = []
    for d in range(9):
        at = jnp.right_shift(node, 9 - d) % 64
        got.append(arrived[pl.ds(pl.multiple_of(at * 16, 16), 16)])
    first = [unpack(got[d][0:8], pick) for d in range(7)]
    second = [unpack(got[d][8:16], pick) for d in (7, 8)]
    z = [first[d][0:16] for d in range(6)]
    z += [first[6][16:32], second[0][0:16], second[1][16:32]]
    zloc = zl[...].astype(F32)
    z.append(zloc[992:1008])
    for i in range(4):
        start = 0 if i == 0 else 112 + 16 * i
        low_rows[start : start + rows[i].shape[0]] = rows[i][...].astype(F32)
    e = []
    for d in range(1, 10):
        at = jnp.right_shift(node, 9 - d)
        e.append(low_rows[pl.ds(at if d < 7 else 16 * d + at % 16 + 16, 1)])

    def spread_down(y, row):
        return jnp.concatenate([y * row[:, 128 * m : 128 * m + 128] for m in range(8)], 1)

    y = z[0]
    for d in range(1, 10):
        t = spread_down(y, e[d - 1]).astype(BF16)
        y = (dot(t, gather) + z[d]).astype(BF16).astype(F32)
    e = transfer[...].astype(F32)
    for h in range(LEVELS - 2, -1, -1):
        n = LPD >> h
        t = [
            spread_down(y[16 * (j // 2) : 16 * (j // 2) + 16], e[OFFS[h] + j : OFFS[h] + j + 1])
            for j in range(n)
        ]
        t = jnp.concatenate(t, 0).astype(BF16)
        zs = zloc[16 * OFFS[h] : 16 * (OFFS[h] + n)]
        y = (dot(t, gather) + zs).astype(BF16).astype(F32)
    bas = basis[...].astype(F32)
    g = lanes((16, 128), 32)
    for i in range(8):
        t = y[64 * i : 64 * i + 16]
        for k in range(1, 4):
            t = jnp.where(g == k, y[64 * i + 16 * k : 64 * i + 16 * k + 16], t)
        s = slice(256 * i, 256 * i + 256)
        far = dot(t.astype(BF16), block_basis(bas, i).astype(BF16))
        out[:, s] = (far + near[:, s]).astype(BF16)


def call(body, out, out_kinds, scratch, kinds, args, micros, parts=()):
    spaces = {"s": pltpu.SMEM, "v": pltpu.VMEM, "h": pltpu.HBM, "p": pltpu.HBM, "d": pltpu.HBM}
    held = []
    for a, k in zip(args, kinds):
        if k == "h":
            held.append(a)
        elif k == "p":
            held += [jax.ShapeDtypeStruct((rows, a.shape[1]), a.dtype) for _, rows in parts]
    sent = [o for o, k in zip(out, out_kinds) if k == "h"]

    def kernel(*refs):
        ins, outs = refs[: len(args)], refs[len(args) : len(args) + len(out)]
        rest = list(refs[len(args) + len(out) :])
        own, rest = rest[: len(scratch)], rest[len(scratch) :]
        sems = rest.pop()
        copies, given, back = [], [], []
        for r, k in zip(ins, kinds):
            if k == "h":
                v = rest.pop(0)
                copies.append(pltpu.make_async_copy(r, v, sems.at[len(copies)]))
                given.append(v)
            elif k == "p":
                blocks = []
                for first, rows in parts:
                    v = rest.pop(0)
                    at = first(*position()) if callable(first) else first
                    at = pl.multiple_of(at, 16) if callable(first) else at
                    src = r.at[pl.ds(at, rows)]
                    copies.append(pltpu.make_async_copy(src, v, sems.at[len(copies)]))
                    blocks.append(v)
                given.append(blocks)
            elif k != "d":
                given.append(r)
        for r, k in zip(outs, out_kinds):
            if k == "h":
                v = rest.pop(0)
                back.append(pltpu.make_async_copy(v, r, sems.at[len(copies) + len(back)]))
                given.append(v)
            else:
                given.append(r)
        for c in copies:
            c.start()

        def ready():
            for c in copies:
                c.wait()

        body(ready, *given, *own)
        for c in back:
            c.start()
        for c in back:
            c.wait()

    buffers = [pltpu.VMEM(a.shape, a.dtype) for a in held + sent]
    return pl.pallas_call(
        kernel,
        out_shape=out,
        in_specs=[pl.BlockSpec(memory_space=spaces[k]) for k in kinds],
        out_specs=[pl.BlockSpec(memory_space=spaces[k]) for k in out_kinds],
        scratch_shapes=list(scratch) + buffers + [pltpu.SemaphoreType.DMA((16,))],
        compiler_params=pltpu.CompilerParams(vmem_limit_bytes=VMEM_LIMIT),
        cost_estimate=pl.CostEstimate(
            flops=int(micros * 1e12), bytes_accessed=int(micros * 3.5e6), transcendentals=0
        ),
    )(*args)


def shape(rows, cols, dtype=BF16):
    return jax.ShapeDtypeStruct((rows, cols), dtype)


def local(
    points,
    basis,
    transfer,
    top_transfer,
    coupling,
    far_index,
    far_count,
    top_coupling,
    top_index,
    top_count,
    near_block,
    near_index,
    near_count,
):
    devices = 512

    root_msg, stack = call(
        up_kernel,
        [shape(512, 128), shape(1024, 128)],
        "hh",
        [],
        "hhh",
        (points, basis, transfer),
        COST[0],
    )
    plane_roots = lax.all_to_all(root_msg, PLANE, 0, 0, tiled=True)
    (ex,) = call(exchange_kernel, [shape(512, 128)], "h", [], "hh", (stack, points), COST[1])
    before = lax.ppermute(ex, ALL, [(i, i + 1) for i in range(devices - 1)])
    after = lax.ppermute(ex, ALL, [(i + 1, i) for i in range(devices - 1)])

    msg, own = call(
        plane_kernel,
        [shape(8 * MSG, 128), shape(896, 128)],
        "hh",
        [pltpu.VMEM((128, 1024), F32)],
        "sshphd",
        (top_index, top_count, plane_roots, top_transfer, top_coupling, ex),
        COST[2],
        parts=[
            (0, 128),
            (lambda y, low: 128 + 16 * y, 16),
            (lambda y, low: 256 + 32 * y, 32),
            (lambda y, low: 512 + 64 * y, 64),
        ],
    )
    planes = lax.all_to_all(msg, "y", 0, 0, tiled=True)

    (z_msg,) = call(
        top_kernel,
        [shape(1024, 128)],
        "h",
        [pltpu.VMEM((NODES * 16, 128), F32)],
        "hhp",
        (planes, own, top_transfer),
        COST[3],
        parts=[(0, 16)],
    )
    z_all = lax.all_to_all(z_msg, PLANE, 0, 0, tiled=True)
    zl, near = call(
        side_kernel,
        [shape(1024, 128), shape(VEC, LPD * LEAF, F32)],
        "hh",
        [
            pltpu.VMEM((3072, 128), F32),
            pltpu.VMEM((1024, 1024), BF16),
            pltpu.VMEM((3104, 128), BF16),
            pltpu.VMEM((512, 256), BF16),
        ],
        "sssshhhhhh",
        (
            far_index,
            far_count,
            near_index,
            near_count,
            before,
            stack,
            after,
            points,
            coupling,
            near_block,
        ),
        COST[4],
    )
    (result,) = call(
        down_kernel,
        [shape(VEC, LPD * LEAF)],
        "h",
        [pltpu.VMEM((176, 1024), F32)],
        "hphhhh",
        (z_all, top_transfer, zl, transfer, basis, near),
        COST[6],
        parts=[
            (0, 128),
            (lambda y, low: 128 + (y * 64 + low) // 4 // 16 * 16, 16),
            (lambda y, low: 256 + (y * 64 + low) // 2 // 16 * 16, 16),
            (lambda y, low: 512 + (y * 64 + low) // 16 * 16, 16),
        ],
    )
    return result


def solution(mesh):
    grid = Mesh(mesh.devices.reshape(8, 8, 2, 4), ALL)
    one, two, three = P(ALL), P(ALL, None), P(ALL, None, None)
    wide = P(None, ALL)
    placed = (wide, wide, two, P(), three, two, one, three, two, one, three, two, one)
    return jax.shard_map(local, mesh=grid, in_specs=placed, out_specs=wide, check_vma=False)
```

```python
import jax
import jax.numpy as jnp
import numpy as np
from jax import lax
from jax.experimental import pallas as pl
from jax.experimental.pallas import tpu as pltpu
from jax.sharding import Mesh
from jax.sharding import PartitionSpec as P

RANK = 32
LEAF = 64
VEC = 16
FAR = 4
NEAR = 4
LPD = 32
LEVELS = 6
OFFS = [2 * LPD - 2 * (LPD >> h) for h in range(LEVELS)]
ALL = ("y", "z", "core", "x")
PLANE = ("z", "core", "x")
REACH = 3
TAPS = 2 * REACH + 1
MSG = 128
SIZES = [(1 << d) + 2 * REACH for d in range(6)] + [8 + 6, 16 + 6, 32 + 6]
STARTS = [sum(SIZES[:d]) for d in range(9)]
NODES = sum(SIZES)
VMEM_LIMIT = 32 << 20
COST = (4, 1, 4, 3, 8, 4, 4)
F32 = jnp.float32
BF16 = jnp.bfloat16

_l = np.arange(128)
def dot(a, b):
    return jnp.dot(a, b, preferred_element_type=F32)


def lanes(shape, width):
    return lax.broadcasted_iota(jnp.int32, shape, len(shape) - 1) // width


def up_level(c, e, spread, n):
    x = dot(c, spread)
    out = []
    row = (lambda i: e[i]) if isinstance(e, list) else (lambda i: e[i : i + 1])
    for p in range(n // 2):
        t = x[32 * p : 32 * p + 16] * row(2 * p)
        t = t + x[32 * p + 16 : 32 * p + 32] * row(2 * p + 1)
        q = t[:, 0:128]
        for m in range(1, 8):
            q = q + t[:, 128 * m : 128 * m + 128]
        out.append(q)
    q = jnp.concatenate(out, 0) if len(out) > 1 else out[0]
    return q.astype(BF16)


def up_levels(c, rows):
    first, rest, fold = spread_matrix(False), spread_matrix(True), fold_matrix()
    levels = []
    n = c.shape[0] // 16
    for i, e in enumerate(rows):
        c = up_level(c, e, first if i == 0 else rest, n)
        levels.append(dot(c, fold).astype(BF16))
        n //= 2
    return levels


def pack(c):
    m = c.shape[0] // 32
    c = c.reshape(m, 4, 8, 128)
    g = lanes((m, 8, 128), 32)
    r = jnp.where(
        g == 0, c[:, 0], jnp.where(g == 1, c[:, 1], jnp.where(g == 2, c[:, 2], c[:, 3]))
    )
    return r.reshape(m * 8, 128)


def unpack(r, pick):
    m = r.shape[0] // 8
    w = dot(r, pick)
    parts = [w[:, 128 * q : 128 * q + 128].reshape(m, 1, 8, 128) for q in range(4)]
    return jnp.concatenate(parts, 1).reshape(m * 32, 128)


def block_basis(basis, i):
    b = basis[:, 256 * i : 256 * i + 256]
    b = jnp.concatenate([b] * 4, 0)
    rows = lax.broadcasted_iota(jnp.int32, (128, 256), 0) // 32
    return jnp.where(rows == lanes((128, 256), 64), b, jnp.zeros_like(b))


def iota(shape, axis, width):
    return lax.broadcasted_iota(jnp.int32, shape, axis) // width


def mask(cond):
    return jnp.where(cond, 1.0, 0.0).astype(BF16)


def spread_matrix(parts):
    r = iota((128, 1024), 0, 1)
    return mask(iota((128, 1024), 1, 32) == (r % 32 if parts else r))


def fold_matrix():
    return mask((iota((128, 128), 1, 1) - iota((128, 128), 0, 1)) % 32 == 0)


def gather_matrix():
    return mask((iota((1024, 128), 0, 32) - iota((1024, 128), 1, 1)) % 32 == 0)


def pick_matrix():
    r, c = iota((128, 512), 0, 1), iota((128, 512), 1, 1)
    return mask(((r - c) % 32 == 0) & (r // 32 == c // 128))


def pair_matrix():
    r, c = iota((256, 128), 0, 1), iota((256, 128), 1, 1)
    return mask(r % 128 // 4 * 2 + r // 128 == c % 64)


def position():
    low = (lax.axis_index("z") * 2 + lax.axis_index("core")) * 4 + lax.axis_index("x")
    return lax.axis_index("y"), low


def up_kernel(ready, points, basis, transfer, root_out, stack_out):
    fold = fold_matrix()
    ready()
    pts = points[...]
    bas = basis[...].astype(F32)
    e = transfer[...].astype(F32)
    rows = []
    g = lanes((16, 128), 32)
    for i in range(8):
        bd = block_basis(bas, i).astype(BF16)
        c = lax.dot_general(
            pts[:, 256 * i : 256 * i + 256],
            bd,
            (((1,), (1,)), ((), ())),
            preferred_element_type=F32,
        )
        for k in range(4):
            rows.append(jnp.where(g == k, c, 0.0))
    c = dot(jnp.concatenate(rows, 0).astype(BF16), fold).astype(BF16)
    below = [e[OFFS[h] : OFFS[h] + (LPD >> h)] for h in range(LEVELS - 1)]
    levels = [c] + up_levels(c, below)
    root = levels[-1].astype(F32)
    g8 = lanes((8, 128), 32)
    msg = jnp.where(g8 == 0, root[0:8], jnp.where(g8 == 1, root[8:16], 0.0))
    msg = jnp.concatenate([msg, msg], 0).astype(BF16)
    for i in range(32):
        root_out[16 * i : 16 * i + 16] = msg
    stack_out[...] = jnp.concatenate(levels + [jnp.zeros((16, 128), BF16)], 0)


def exchange_kernel(ready, stack, points, ex_out, chain_out, rows, low_rows):
    ready()
    ex_out[0:256] = pack(stack[...].astype(F32)).astype(BF16)
    for i in range(16):
        ex_out[256 + 16 * i : 272 + 16 * i] = points[:, 128 * i : 128 * i + 128]
    y, low = position()
    node = 512 + y * 64 + low
    one, rest, fold = spread_matrix(False), spread_matrix(True), fold_matrix()
    q = mask(iota((32, 128), 0, 1) == iota((32, 128), 1, 1))
    for c in ready.rest:
        c.wait()
    ready.rest.clear()
    low_rows[0:128] = rows[0:128].astype(F32)
    low_rows[128:176] = rows[240:288].astype(F32)
    for d in range(9, 0, -1):
        at = jnp.right_shift(node, 9 - d)
        t = dot(q, one if d == 9 else rest)
        t = t * low_rows[pl.ds(at if d < 7 else 16 * d + at % 16 + 16, 1)]
        p = t[:, 0:128]
        for m in range(1, 8):
            p = p + t[:, 128 * m : 128 * m + 128]
        q = p.astype(BF16)
        g = dot(q, fold).astype(BF16)
        chain_out[:, 128 * (d - 1) : 128 * d] = jnp.concatenate([g] * 4, 0)


def plane_kernel(
    ready, index, count, arrived, rows, tops, msg_out, own_out, low_rows
):
    pick = pick_matrix()
    y, low = position()
    node = y * 64 + low
    ready()
    w = dot(arrived[...], pick[:, 0:256])
    c = jnp.concatenate(
        [w[:, 0:128].reshape(64, 1, 8, 128), w[:, 128:256].reshape(64, 1, 8, 128)], 1
    )
    c = c.reshape(1024, 128).astype(BF16)
    low_rows[...] = rows[0:128].astype(F32)
    e = [rows[176:240].astype(F32), rows[144:176].astype(F32), rows[128:144].astype(F32)]
    e.append(low_rows[pl.ds(pl.multiple_of(64 + 8 * y, 8), 8)])
    for n in (4, 2):
        e.append([low_rows[pl.ds(8 * n + n * y + i, 1)] for i in range(n)])
    levels = up_levels(c, e)
    d8, d7, d6, d5, d4, d3 = levels
    own_out[0:128] = d6
    own_out[128:384] = d7
    own_out[384:896] = d8
    inner = [d3, d4, d5]
    first = pack(jnp.concatenate(inner + [d6[0:48], d7[0:48], d8[0:48]], 0).astype(F32))
    last = pack(jnp.concatenate(inner + [d6[80:128], d7[208:256], d8[464:512]], 0).astype(F32))
    b = tops[0].astype(F32)
    taps = jnp.zeros((8, 1024), F32)
    for f in range(FAR):
        tap = index[0, f] - node + REACH
        tap = jnp.where((f < count[0]) & (node > 0), tap, -1)
        taps = taps + jnp.where(iota((8, 1024), 0, 1) == tap, b[f : f + 1], 0.0)
    taps = [taps[:, 128 * m : 128 * m + 128] for m in range(8)]
    taps = jnp.concatenate(taps, 0).astype(BF16)
    for p in range(8):
        msg_out[MSG * p : MSG * p + 64] = taps
        msg_out[MSG * p + 64 : MSG * p + 128] = jnp.where(y < p, last, first).astype(BF16)


def top_kernel(ready, arrived, own, rows, out, table):
    pick, gather = pick_matrix(), gather_matrix()
    y, low = position()
    depth = sum((low >= (1 << d)).astype(jnp.int32) for d in range(1, 6))
    start, first = jnp.int32(STARTS[0]), jnp.int32(0)
    for d in range(6):
        start = jnp.where(depth == d, STARTS[d], start)
        first = jnp.where((depth == d) & (low > 0), 1 << d, first)
    planes = (0, 1, 2 + y // 4, 4 + y // 2)
    places = (start + low - first, STARTS[6] + low % 8, STARTS[7] + low % 16, STARTS[8] + low % 32)
    table[...] = jnp.zeros((NODES * 16, 128), F32)
    ready()

    def put(depth, place, value):
        s = (STARTS[depth] + place) * 16
        table[s : s + value.shape[0]] = value

    d3 = []
    for p in range(8):
        c = unpack(arrived[MSG * p + 64 : MSG * p + 96], pick)
        d3.append(c[0:16])
        put(4, REACH + 2 * p, c[16:48])
        put(5, REACH + 4 * p, c[48:112])
    c = jnp.concatenate(d3, 0)
    put(3, REACH, c)
    c = c.astype(BF16)
    e = rows[...].astype(F32)
    for d, c in zip((2, 1, 0), up_levels(c, [e[8:16], e[4:8], e[2:4]])):
        put(d, REACH, c.astype(F32))
    prior = unpack(arrived[pl.ds(pl.multiple_of(jnp.maximum(y - 1, 0) * MSG, 16), MSG)][64:128], pick)
    later = unpack(arrived[pl.ds(pl.multiple_of(jnp.minimum(y + 1, 7) * MSG, 16), MSG)][64:128], pick)
    mine = own[...].astype(F32)
    for i, n in enumerate((8, 16, 32)):
        put(6 + i, REACH + n, later[16 * (7 + 3 * i) : 16 * (10 + 3 * i)])
        put(6 + i, 0, prior[16 * (7 + 3 * i) : 16 * (10 + 3 * i)])
        begin = 16 * (n - 8)
        put(6 + i, REACH, mine[begin : begin + 16 * n])
    sums = []
    for s in range(4):
        taps = arrived[pl.ds(pl.multiple_of(planes[s] * MSG, 16), MSG)][0:64].astype(F32)
        acc = [None] * 8
        for o in range(TAPS):
            c = table[pl.ds(pl.multiple_of((places[s] + o) * 16, 16), 16)]
            for m in range(8):
                t = taps[8 * m + o : 8 * m + o + 1] * c
                acc[m] = t if o == 0 else acc[m] + t
        sums.append(jnp.concatenate(acc, 1))
    z = dot(jnp.concatenate(sums, 0).astype(BF16), gather)
    z = pack(z).astype(BF16)
    for i in range(64):
        out[16 * i : 16 * i + 16] = z


def side_kernel(
    ready,
    far_index,
    far_count,
    near_index,
    near_count,
    before,
    stack,
    after,
    points,
    coupling,
    block,
    zl_out,
    near_out,
    table,
    prod,
    leaves,
    halves,
):
    pick, gather, pair = pick_matrix(), gather_matrix(), pair_matrix()
    y, low = position()
    prior = y * 64 + low - 1
    prod[1008:1024] = jnp.zeros((16, 1024), BF16)
    ready()

    window = [before[256:512]]
    window += [points[:, 128 * i : 128 * i + 128] for i in range(16)]
    window += [after[256:512]]
    w = jnp.concatenate(window, 0).astype(F32)
    turned = jnp.concatenate([w[:, 64:128], w[:, 0:64]], 1)
    left = lanes((768, 128), 64) == 0
    four = [
        jnp.where(left, w, 0.0),
        jnp.where(left, 0.0, turned),
        jnp.where(left, turned, 0.0),
        jnp.where(left, 0.0, w),
    ]
    four = jnp.concatenate([x.reshape(48, 1, 16, 128) for x in four], 1)
    leaves[0:3072] = four.reshape(3072, 128).astype(BF16)
    leaves[3072:3104] = jnp.zeros((32, 128), BF16)
    slot = lanes((32, 128), 1) % NEAR

    def leaf(t):
        b = block[t].astype(F32)
        mat = jnp.concatenate([b[:, 128 * m : 128 * m + 128] for m in range(32)], 0)
        vec = []
        for f in range(NEAR):
            at = near_index[t, f] - prior * LPD
            at = jnp.where(f < near_count[t], at, 3 * LPD) * 32
            vec.append(leaves[pl.ds(pl.multiple_of(at, 32), 32)])
        r = lax.dot_general(
            jnp.concatenate(vec, 0),
            mat.astype(BF16),
            (((1,), (1,)), ((), ())),
            preferred_element_type=F32,
        )
        q = jnp.where(slot == 0, r[0:32], 0.0)
        for f in range(1, NEAR):
            q = jnp.where(slot == f, r[32 * f : 32 * f + 32], q)
        q = q.astype(BF16)
        at = pl.ds(pl.multiple_of(t * 16, 16), 16)
        halves[at, 0:128] = q[0:16]
        halves[at, 128:256] = q[16:32]

    pl.loop(0, LPD, unroll=4)(leaf)
    r = dot(halves[...], pair)
    g = lanes((16, 128), 64)
    for i in range(16):
        near_out[:, 128 * i : 128 * i + 128] = jnp.where(
            g == 0, r[32 * i : 32 * i + 16], r[32 * i + 16 : 32 * i + 32]
        )

    table[0:1024] = unpack(before[0:256], pick)
    table[1024:2048] = stack[...].astype(F32)
    table[2048:3072] = unpack(after[0:256], pick)

    def level(h):
        n = LPD >> h

        def step(t):
            b = coupling[t].astype(F32)
            acc = [None] * 8
            for f in range(FAR):
                at = far_index[t, f] - prior * n
                at = at + OFFS[h] + (64 - n) * (
                    (at >= n).astype(jnp.int32) + (at >= 2 * n).astype(jnp.int32)
                )
                at = jnp.where(f < far_count[t], at, 127) * 16
                c = table[pl.ds(pl.multiple_of(at, 16), 16)]
                for m in range(8):
                    r = b[f : f + 1, 128 * m : 128 * m + 128] * c
                    acc[m] = r if f == 0 else acc[m] + r
            prod[pl.ds(pl.multiple_of(t * 16, 16), 16)] = jnp.concatenate(acc, 1).astype(BF16)

        pl.loop(OFFS[h], OFFS[h] + n, unroll=min(n, 4))(step)

    for h in range(LEVELS):
        level(h)
    zl_out[...] = dot(prod[...], gather).astype(BF16)


def down_kernel(ready, arrived, chain, zl, transfer, basis, near, out):
    gather = gather_matrix()
    y, low = position()
    node = 512 + y * 64 + low
    ready()
    parts = []
    g = lanes((8, 128), 32)
    for d in range(9):
        at = jnp.right_shift(node, 9 - d) % 64
        got = arrived[pl.ds(pl.multiple_of(at * 16, 16), 16)].astype(F32)
        got = got[0:8] if d < 7 else got[8:16]
        q = 2 if d in (6, 8) else 0
        parts.append(
            jnp.concatenate([jnp.where(g == q, got, 0.0), jnp.where(g == q + 1, got, 0.0)], 0)
        )
    y = lax.dot_general(
        jnp.concatenate(parts, 1).astype(BF16),
        chain[...],
        (((1,), (1,)), ((), ())),
        preferred_element_type=F32,
    )
    zloc = zl[...].astype(F32)
    y = (y + zloc[992:1008]).astype(BF16).astype(F32)

    def spread_down(y, row):
        return jnp.concatenate([y * row[:, 128 * m : 128 * m + 128] for m in range(8)], 1)

    e = transfer[...].astype(F32)
    for h in range(LEVELS - 2, -1, -1):
        n = LPD >> h
        t = [
            spread_down(y[16 * (j // 2) : 16 * (j // 2) + 16], e[OFFS[h] + j : OFFS[h] + j + 1])
            for j in range(n)
        ]
        t = jnp.concatenate(t, 0).astype(BF16)
        zs = zloc[16 * OFFS[h] : 16 * (OFFS[h] + n)]
        y = (dot(t, gather) + zs).astype(BF16).astype(F32)
    bas = basis[...].astype(F32)
    g = lanes((16, 128), 32)
    for i in range(8):
        t = y[64 * i : 64 * i + 16]
        for k in range(1, 4):
            t = jnp.where(g == k, y[64 * i + 16 * k : 64 * i + 16 * k + 16], t)
        s = slice(256 * i, 256 * i + 256)
        far = dot(t.astype(BF16), block_basis(bas, i).astype(BF16))
        out[:, s] = (far + near[:, s]).astype(BF16)


def call(body, out, out_kinds, scratch, kinds, args, micros, direct=()):
    spaces = {"s": pltpu.SMEM, "v": pltpu.VMEM, "w": pltpu.VMEM, "h": pltpu.HBM, "r": pltpu.HBM}
    held = [a for a, k in zip(args, kinds) if k == "h"]
    sent = [o for o, k in zip(out, out_kinds) if k == "h"]

    def kernel(*refs):
        ins, outs = refs[: len(args)], refs[len(args) : len(args) + len(out)]
        rest = list(refs[len(args) + len(out) :])
        own, rest = rest[: len(scratch)], rest[len(scratch) :]
        sems = rest.pop()
        copies, given, back, straight = [], [], [], []
        for r, k in zip(ins, kinds):
            if k == "h":
                v = rest.pop(0)
                copies.append(pltpu.make_async_copy(r, v, sems.at[len(copies)]))
                given.append(v)
            elif k != "r":
                given.append(r)
        for r, k in zip(outs, out_kinds):
            if k == "h":
                v = rest.pop(0)
                back.append(pltpu.make_async_copy(v, r, sems.at[len(copies) + len(back)]))
                given.append(v)
            elif k != "r":
                given.append(r)
        for i, first, rows, o, to in direct:
            src, dst = ins[i], outs[o]
            if rows:
                at = first(*position()) if callable(first) else first
                at = pl.multiple_of(at, 16) if callable(first) else at
                src, dst = src.at[pl.ds(at, rows)], dst.at[pl.ds(to, rows)]
            sem = sems.at[len(copies) + len(back) + len(straight)]
            straight.append(pltpu.make_async_copy(src, dst, sem))
        for c in copies + straight:
            c.start()

        def ready():
            for c in copies:
                c.wait()

        ready.rest = straight
        body(ready, *given, *own)
        for c in back:
            c.start()
        for c in back + straight:
            c.wait()

    buffers = [pltpu.VMEM(a.shape, a.dtype) for a in held + sent]
    return pl.pallas_call(
        kernel,
        out_shape=[
            (pltpu.HBM if k == "h" else pltpu.VMEM)(o.shape, o.dtype)
            for o, k in zip(out, out_kinds)
        ],
        in_specs=[pl.BlockSpec(memory_space=spaces[k]) for k in kinds],
        out_specs=[
            pl.BlockSpec(memory_space=pltpu.HBM if k == "h" else pltpu.VMEM) for k in out_kinds
        ],
        scratch_shapes=list(scratch) + buffers + [pltpu.SemaphoreType.DMA((24,))],
        compiler_params=pltpu.CompilerParams(vmem_limit_bytes=VMEM_LIMIT),
        cost_estimate=pl.CostEstimate(
            flops=int(micros * 1e12), bytes_accessed=int(micros * 3.5e6), transcendentals=0
        ),
    )(
        *[
            pltpu.with_memory_space_constraint(a, spaces[k]) if k in "whr" else a
            for a, k in zip(args, kinds)
        ]
    )


def shape(rows, cols, dtype=BF16):
    return jax.ShapeDtypeStruct((rows, cols), dtype)


def local(
    points,
    basis,
    transfer,
    top_transfer,
    coupling,
    far_index,
    far_count,
    top_coupling,
    top_index,
    top_count,
    near_block,
    near_index,
    near_count,
):
    devices = 512

    def like(*arrays):
        return [jax.ShapeDtypeStruct(a.shape, a.dtype) for a in arrays]

    root_msg, stack = call(
        up_kernel,
        [shape(512, 128), shape(1024, 128)],
        "hh",
        [],
        "hhh",
        (points, basis, transfer),
        COST[0],
    )
    plane_roots = lax.all_to_all(root_msg, PLANE, 0, 0, tiled=True)

    ex, chain, rows, tops = call(
        exchange_kernel,
        [shape(512, 128), shape(128, 1152), shape(288, 1024)] + like(top_coupling),
        "hhqr",
        [pltpu.VMEM((176, 1024), F32)],
        "hhrr",
        (stack, points, top_transfer, top_coupling),
        COST[1],
        direct=[
            (2, 0, 128, 2, 0),
            (2, lambda y, low: 128 + (y * 64 + low) // 4 // 16 * 16, 16, 2, 240),
            (2, lambda y, low: 256 + (y * 64 + low) // 2 // 16 * 16, 16, 2, 256),
            (2, lambda y, low: 512 + (y * 64 + low) // 16 * 16, 16, 2, 272),
            (2, lambda y, low: 512 + 64 * y, 64, 2, 176),
            (2, lambda y, low: 256 + 32 * y, 32, 2, 144),
            (2, lambda y, low: 128 + 16 * y, 16, 2, 128),
            (3, 0, 0, 3, 0),
        ],
    )
    before = lax.ppermute(ex, ALL, [(i, i + 1) for i in range(devices - 1)])
    after = lax.ppermute(ex, ALL, [(i + 1, i) for i in range(devices - 1)])

    msg, own, first_rows = call(
        plane_kernel,
        [shape(8 * MSG, 128), shape(896, 128), shape(16, 1024)],
        "hvr",
        [pltpu.VMEM((128, 1024), F32)],
        "sswvvr",
        (top_index, top_count, plane_roots, rows, tops, top_transfer),
        COST[2],
        direct=[(5, 0, 16, 2, 0)],
    )
    planes = lax.all_to_all(msg, "y", 0, 0, tiled=True)
    (z_msg,) = call(
        top_kernel,
        [shape(1024, 128)],
        "h",
        [pltpu.VMEM((NODES * 16, 128), F32)],
        "wvv",
        (planes, own, first_rows),
        COST[3],
    )
    z_all = lax.all_to_all(z_msg, PLANE, 0, 0, tiled=True)
    zl, near, held_chain, held_transfer, held_basis = call(
        side_kernel,
        [shape(1024, 128), shape(VEC, LPD * LEAF, F32)] + like(chain, transfer, basis),
        "vvrrr",
        [
            pltpu.VMEM((3072, 128), F32),
            pltpu.VMEM((1024, 1024), BF16),
            pltpu.VMEM((3104, 128), BF16),
            pltpu.VMEM((512, 256), BF16),
        ],
        "sssswhwhhhrrr",
        (
            far_index,
            far_count,
            near_index,
            near_count,
            before,
            stack,
            after,
            points,
            coupling,
            near_block,
            chain,
            transfer,
            basis,
        ),
        COST[4],
        direct=[(10, 0, 0, 2, 0), (11, 0, 0, 3, 0), (12, 0, 0, 4, 0)],
    )
    (result,) = call(
        down_kernel,
        [shape(VEC, LPD * LEAF)],
        "h",
        [],
        "wvvvvv",
        (z_all, held_chain, zl, held_transfer, held_basis, near),
        COST[6],
    )
    return result


def solution(mesh):
    grid = Mesh(mesh.devices.reshape(8, 8, 2, 4), ALL)
    one, two, three = P(ALL), P(ALL, None), P(ALL, None, None)
    wide = P(None, ALL)
    placed = (wide, wide, two, P(), three, two, one, three, two, one, three, two, one)
    return jax.shard_map(local, mesh=grid, in_specs=placed, out_specs=wide, check_vma=False)
```

```python
import jax
import jax.numpy as jnp
import numpy as np
from jax import lax
from jax.experimental import pallas as pl
from jax.experimental.pallas import tpu as pltpu
from jax.sharding import Mesh
from jax.sharding import PartitionSpec as P

RANK = 32
LEAF = 64
VEC = 16
FAR = 4
NEAR = 4
LPD = 32
LEVELS = 6
OFFS = [2 * LPD - 2 * (LPD >> h) for h in range(LEVELS)]
ALL = ("y", "z", "core", "x")
PLANE = ("z", "core", "x")
REACH = 3
TAPS = 2 * REACH + 1
MSG = 128
SIZES = [(1 << d) + 2 * REACH for d in range(6)] + [8 + 6, 16 + 6, 32 + 6]
STARTS = [sum(SIZES[:d]) for d in range(9)]
NODES = sum(SIZES)
VMEM_LIMIT = 32 << 20
COST = (4, 1, 4, 3, 8, 4, 4)
F32 = jnp.float32
BF16 = jnp.bfloat16

_l = np.arange(128)
def dot(a, b):
    return jnp.dot(a, b, preferred_element_type=F32)


def lanes(shape, width):
    return lax.broadcasted_iota(jnp.int32, shape, len(shape) - 1) // width


def up_level(c, e, spread, n):
    x = dot(c, spread)
    out = []
    row = (lambda i: e[i]) if isinstance(e, list) else (lambda i: e[i : i + 1])
    for p in range(n // 2):
        t = x[32 * p : 32 * p + 16] * row(2 * p)
        t = t + x[32 * p + 16 : 32 * p + 32] * row(2 * p + 1)
        q = t[:, 0:128]
        for m in range(1, 8):
            q = q + t[:, 128 * m : 128 * m + 128]
        out.append(q)
    q = jnp.concatenate(out, 0) if len(out) > 1 else out[0]
    return q.astype(BF16)


def up_levels(c, rows):
    spread, fold = spread_matrix(), fold_matrix()
    levels = []
    n = c.shape[0] // 16
    for e in rows:
        c = up_level(c, e, spread, n)
        levels.append(dot(c, fold).astype(BF16))
        n //= 2
    return levels


def pack(c):
    m = c.shape[0] // 32
    c = c.reshape(m, 4, 8, 128)
    g = lanes((m, 8, 128), 32)
    r = jnp.where(
        g == 0, c[:, 0], jnp.where(g == 1, c[:, 1], jnp.where(g == 2, c[:, 2], c[:, 3]))
    )
    return r.reshape(m * 8, 128)


def unpack(r, pick):
    m = r.shape[0] // 8
    w = dot(r, pick)
    parts = [w[:, 128 * q : 128 * q + 128].reshape(m, 1, 8, 128) for q in range(4)]
    return jnp.concatenate(parts, 1).reshape(m * 32, 128)


def down_levels(y, e, added, gather):
    v = y.shape[0]
    for h in range(LEVELS - 2, -1, -1):
        n = LPD >> h
        t = []
        for j in range(n):
            p = y[v * (j // 2) : v * (j // 2) + v]
            row = e[OFFS[h] + j : OFFS[h] + j + 1]
            t.append(
                jnp.concatenate([p * row[:, 128 * m : 128 * m + 128] for m in range(8)], 1).astype(
                    BF16
                )
            )
        y = dot(jnp.concatenate(t, 0), gather)
        if added is not None:
            y = y + added[v * OFFS[h] : v * (OFFS[h] + n)]
        y = y.astype(BF16).astype(F32)
    return y


def at_points(y, basis):
    v = y.shape[0] // LPD
    g = lanes((v, 128), 32)
    out = []
    for i in range(8):
        t = y[4 * v * i : 4 * v * i + v]
        for k in range(1, 4):
            t = jnp.where(g == k, y[4 * v * i + v * k : 4 * v * i + v * k + v], t)
        out.append(dot(t.astype(BF16), block_basis(basis, i).astype(BF16)))
    return out


def block_basis(basis, i):
    b = basis[:, 256 * i : 256 * i + 256]
    b = jnp.concatenate([b] * 4, 0)
    rows = lax.broadcasted_iota(jnp.int32, (128, 256), 0) // 32
    return jnp.where(rows == lanes((128, 256), 64), b, jnp.zeros_like(b))


def iota(shape, axis, width):
    return lax.broadcasted_iota(jnp.int32, shape, axis) // width


def mask(cond):
    return jnp.where(cond, 1.0, 0.0).astype(BF16)


def spread_matrix():
    return mask(iota((128, 1024), 1, 32) == iota((128, 1024), 0, 1) % 32)


def fold_matrix():
    return mask((iota((128, 128), 1, 1) - iota((128, 128), 0, 1)) % 32 == 0)


def gather_matrix():
    return mask((iota((1024, 128), 0, 32) - iota((1024, 128), 1, 1)) % 32 == 0)


def pick_matrix():
    r, c = iota((128, 512), 0, 1), iota((128, 512), 1, 1)
    return mask(((r - c) % 32 == 0) & (r // 32 == c // 128))


def pair_matrix():
    r, c = iota((256, 128), 0, 1), iota((256, 128), 1, 1)
    return mask(r % 128 // 4 * 2 + r // 128 == c % 64)


def position():
    low = (lax.axis_index("z") * 2 + lax.axis_index("core")) * 4 + lax.axis_index("x")
    return lax.axis_index("y"), low


def up_kernel(ready, points, basis, transfer, root_out, stack_out):
    fold = fold_matrix()
    ready()
    pts = points[...]
    bas = basis[...].astype(F32)
    e = transfer[...].astype(F32)
    rows = []
    g = lanes((16, 128), 32)
    for i in range(8):
        bd = block_basis(bas, i).astype(BF16)
        c = lax.dot_general(
            pts[:, 256 * i : 256 * i + 256],
            bd,
            (((1,), (1,)), ((), ())),
            preferred_element_type=F32,
        )
        for k in range(4):
            rows.append(jnp.where(g == k, c, 0.0))
    c = jnp.concatenate(rows, 0).astype(BF16)
    below = [e[OFFS[h] : OFFS[h] + (LPD >> h)] for h in range(LEVELS - 1)]
    levels = [dot(c, fold).astype(BF16)] + up_levels(c, below)
    root = levels[-1].astype(F32)
    g8 = lanes((8, 128), 32)
    msg = jnp.where(g8 == 0, root[0:8], jnp.where(g8 == 1, root[8:16], 0.0))
    msg = jnp.concatenate([msg, msg], 0).astype(BF16)
    for i in range(32):
        root_out[16 * i : 16 * i + 16] = msg
    stack_out[...] = jnp.concatenate(levels + [jnp.zeros((16, 128), BF16)], 0)


def exchange_kernel(
    ready, stack, points, transfer, basis, ex_out, chain_out, nested_out, rows, low_rows
):
    ready()
    ex_out[0:256] = pack(stack[...].astype(F32)).astype(BF16)
    for i in range(16):
        ex_out[256 + 16 * i : 272 + 16 * i] = points[:, 128 * i : 128 * i + 128]
    y, low = position()
    node = 512 + y * 64 + low
    spread, fold = spread_matrix(), fold_matrix()
    q = mask(iota((32, 128), 0, 1) == iota((32, 128), 1, 1))
    for c in ready.rest:
        c.wait()
    ready.rest.clear()
    low_rows[0:128] = rows[0:128].astype(F32)
    low_rows[128:176] = rows[240:288].astype(F32)
    for d in range(9, 0, -1):
        at = jnp.right_shift(node, 9 - d)
        t = dot(q, spread)
        t = t * low_rows[pl.ds(at if d < 7 else 16 * d + at % 16 + 16, 1)]
        p = t[:, 0:128]
        for m in range(1, 8):
            p = p + t[:, 128 * m : 128 * m + 128]
        q = p.astype(BF16)
        g = dot(q, fold).astype(BF16)
        chain_out[:, 128 * (d - 1) : 128 * d] = jnp.concatenate([g] * 4, 0)
    one = jnp.where((iota((32, 128), 0, 1) - iota((32, 128), 1, 1)) % 32 == 0, 1.0, 0.0)
    leaves = down_levels(one, transfer[...].astype(F32), None, gather_matrix())
    for i, u in enumerate(at_points(leaves, basis[...].astype(F32))):
        nested_out[:, 256 * i : 256 * i + 256] = u.astype(BF16)


def plane_kernel(
    ready, index, count, arrived, rows, tops, msg_out, own_out, low_rows
):
    y, low = position()
    node = y * 64 + low
    ready()
    c = arrived[...].astype(F32).reshape(64, 1, 8, 128)
    g = lanes((64, 1, 8, 128), 32)
    c = jnp.concatenate([jnp.where(g == 0, c, 0.0), jnp.where(g == 1, c, 0.0)], 1)
    c = c.reshape(1024, 128).astype(BF16)
    low_rows[...] = rows[0:128].astype(F32)
    e = [rows[176:240].astype(F32), rows[144:176].astype(F32), rows[128:144].astype(F32)]
    e.append(low_rows[pl.ds(pl.multiple_of(64 + 8 * y, 8), 8)])
    for n in (4, 2):
        e.append([low_rows[pl.ds(8 * n + n * y + i, 1)] for i in range(n)])
    levels = up_levels(c, e)
    d8, d7, d6, d5, d4, d3 = levels
    own_out[0:128] = d6
    own_out[128:384] = d7
    own_out[384:896] = d8
    inner = [d3, d4, d5]
    first = pack(jnp.concatenate(inner + [d6[0:48], d7[0:48], d8[0:48]], 0).astype(F32))
    last = pack(jnp.concatenate(inner + [d6[80:128], d7[208:256], d8[464:512]], 0).astype(F32))
    b = tops[0].astype(F32)
    taps = jnp.zeros((8, 1024), F32)
    for f in range(FAR):
        tap = index[0, f] - node + REACH
        tap = jnp.where((f < count[0]) & (node > 0), tap, -1)
        taps = taps + jnp.where(iota((8, 1024), 0, 1) == tap, b[f : f + 1], 0.0)
    taps = [taps[:, 128 * m : 128 * m + 128] for m in range(8)]
    taps = jnp.concatenate(taps, 0).astype(BF16)
    for p in range(8):
        msg_out[MSG * p : MSG * p + 64] = taps
        msg_out[MSG * p + 64 : MSG * p + 128] = jnp.where(y < p, last, first).astype(BF16)


def top_kernel(ready, arrived, own, rows, out, table):
    pick, gather = pick_matrix(), gather_matrix()
    y, low = position()
    depth = sum((low >= (1 << d)).astype(jnp.int32) for d in range(1, 6))
    start, first = jnp.int32(STARTS[0]), jnp.int32(0)
    for d in range(6):
        start = jnp.where(depth == d, STARTS[d], start)
        first = jnp.where((depth == d) & (low > 0), 1 << d, first)
    planes = (0, 1, 2 + y // 4, 4 + y // 2)
    places = (start + low - first, STARTS[6] + low % 8, STARTS[7] + low % 16, STARTS[8] + low % 32)
    ready()

    def put(depth, place, value):
        s = (STARTS[depth] + place) * 16
        table[s : s + value.shape[0]] = value

    for d in range(6):
        put(d, 0, jnp.zeros((16 * REACH, 128), F32))
        put(d, REACH + (1 << d), jnp.zeros((16 * REACH, 128), F32))
    d3 = []
    for p in range(8):
        c = unpack(arrived[MSG * p + 64 : MSG * p + 96], pick)
        d3.append(c[0:16])
        put(4, REACH + 2 * p, c[16:48])
        put(5, REACH + 4 * p, c[48:112])
    c = jnp.concatenate(d3, 0)
    put(3, REACH, c)
    c = jnp.where(lanes((128, 128), 32) == 0, c, 0.0).astype(BF16)
    e = rows[...].astype(F32)
    for d, c in zip((2, 1, 0), up_levels(c, [e[8:16], e[4:8], e[2:4]])):
        put(d, REACH, c.astype(F32))
    prior = unpack(arrived[pl.ds(pl.multiple_of(jnp.maximum(y - 1, 0) * MSG, 16), MSG)][64:128], pick)
    later = unpack(arrived[pl.ds(pl.multiple_of(jnp.minimum(y + 1, 7) * MSG, 16), MSG)][64:128], pick)
    mine = own[...].astype(F32)
    for i, n in enumerate((8, 16, 32)):
        put(6 + i, REACH + n, later[16 * (7 + 3 * i) : 16 * (10 + 3 * i)])
        put(6 + i, 0, prior[16 * (7 + 3 * i) : 16 * (10 + 3 * i)])
        begin = 16 * (n - 8)
        put(6 + i, REACH, mine[begin : begin + 16 * n])
    sums = []
    for s in range(4):
        taps = arrived[pl.ds(pl.multiple_of(planes[s] * MSG, 16), MSG)][0:64].astype(F32)
        acc = [None] * 8
        for o in range(TAPS):
            c = table[pl.ds(pl.multiple_of((places[s] + o) * 16, 16), 16)]
            for m in range(8):
                t = taps[8 * m + o : 8 * m + o + 1] * c
                acc[m] = t if o == 0 else acc[m] + t
        sums.append(jnp.concatenate(acc, 1))
    z = dot(jnp.concatenate(sums, 0).astype(BF16), gather)
    z = pack(z).astype(BF16)
    for i in range(64):
        out[16 * i : 16 * i + 16] = z


def side_kernel(
    ready,
    far_index,
    far_count,
    near_index,
    near_count,
    before,
    stack,
    after,
    points,
    coupling,
    transfer,
    basis,
    block,
    out,
    table,
    prod,
    leaves,
    halves,
):
    pick, gather, pair = pick_matrix(), gather_matrix(), pair_matrix()
    y, low = position()
    prior = y * 64 + low - 1
    prod[1008:1024] = jnp.zeros((16, 1024), BF16)
    ready(0)
    table[0:1024] = unpack(before[0:256], pick)
    table[1024:2048] = stack[...].astype(F32)
    table[2048:3072] = unpack(after[0:256], pick)
    ready(1)

    window = [before[256:512]]
    window += [points[:, 128 * i : 128 * i + 128] for i in range(16)]
    window += [after[256:512]]
    w = jnp.concatenate(window, 0).astype(F32)
    turned = jnp.concatenate([w[:, 64:128], w[:, 0:64]], 1)
    left = lanes((768, 128), 64) == 0
    four = [
        jnp.where(left, w, 0.0),
        jnp.where(left, 0.0, turned),
        jnp.where(left, turned, 0.0),
        jnp.where(left, 0.0, w),
    ]
    four = jnp.concatenate([x.reshape(48, 1, 16, 128) for x in four], 1)
    leaves[0:3072] = four.reshape(3072, 128).astype(BF16)
    leaves[3072:3104] = jnp.zeros((32, 128), BF16)
    def level(h):
        n = LPD >> h

        def step(t):
            b = coupling[t].astype(F32)
            acc = [None] * 8
            for f in range(FAR):
                at = far_index[t, f] - prior * n
                at = at + OFFS[h] + (64 - n) * (
                    (at >= n).astype(jnp.int32) + (at >= 2 * n).astype(jnp.int32)
                )
                at = jnp.where(f < far_count[t], at, 127) * 16
                c = table[pl.ds(pl.multiple_of(at, 16), 16)]
                for m in range(8):
                    r = b[f : f + 1, 128 * m : 128 * m + 128] * c
                    acc[m] = r if f == 0 else acc[m] + r
            prod[pl.ds(pl.multiple_of(t * 16, 16), 16)] = jnp.concatenate(acc, 1).astype(BF16)

        pl.loop(OFFS[h], OFFS[h] + n, unroll=min(n, 16))(step)

    ready(2)
    for h in range(LEVELS):
        level(h)
    zl = dot(prod[...], gather).astype(BF16).astype(F32)
    ready(3, 4)
    y = down_levels(zl[992:1008], transfer[...].astype(F32), zl, gather)
    far = at_points(y, basis[...].astype(F32))
    ready(5)
    slot = lanes((32, 128), 1) % NEAR

    def leaf(t):
        b = block[t].astype(F32)
        mat = jnp.concatenate([b[:, 128 * m : 128 * m + 128] for m in range(32)], 0)
        vec = []
        for f in range(NEAR):
            at = near_index[t, f] - prior * LPD
            at = jnp.where(f < near_count[t], at, 3 * LPD) * 32
            vec.append(leaves[pl.ds(pl.multiple_of(at, 32), 32)])
        r = lax.dot_general(
            jnp.concatenate(vec, 0),
            mat.astype(BF16),
            (((1,), (1,)), ((), ())),
            preferred_element_type=F32,
        )
        q = jnp.where(slot == 0, r[0:32], 0.0)
        for f in range(1, NEAR):
            q = jnp.where(slot == f, r[32 * f : 32 * f + 32], q)
        q = q.astype(BF16)
        at = pl.ds(pl.multiple_of(t * 16, 16), 16)
        halves[at, 0:128] = q[0:16]
        halves[at, 128:256] = q[16:32]

    pl.loop(0, LPD, unroll=32)(leaf)
    r = dot(halves[...], pair)
    g = lanes((16, 128), 64)
    for i in range(16):
        near = jnp.where(g == 0, r[32 * i : 32 * i + 16], r[32 * i + 16 : 32 * i + 32])
        own = far[i // 2][:, 128 * (i % 2) : 128 * (i % 2) + 128]
        out[:, 128 * i : 128 * i + 128] = near + own


def down_kernel(ready, arrived, chain, nested, rest, out):
    y, low = position()
    node = 512 + y * 64 + low
    ready()
    parts = []
    g = lanes((8, 128), 32)
    for d in range(9):
        at = jnp.right_shift(node, 9 - d) % 64
        got = arrived[pl.ds(pl.multiple_of(at * 16, 16), 16)].astype(F32)
        got = got[0:8] if d < 7 else got[8:16]
        q = 2 if d in (6, 8) else 0
        parts.append(
            jnp.concatenate([jnp.where(g == q, got, 0.0), jnp.where(g == q + 1, got, 0.0)], 0)
        )
    y = lax.dot_general(
        jnp.concatenate(parts, 1).astype(BF16),
        chain[...],
        (((1,), (1,)), ((), ())),
        preferred_element_type=F32,
    )
    y = y[:, 0:RANK].astype(BF16)
    for i in range(8):
        s = slice(256 * i, 256 * i + 256)
        out[:, s] = (dot(y, nested[:, s]) + rest[:, s]).astype(BF16)


def call(body, out, out_kinds, scratch, kinds, args, micros, direct=()):
    spaces = {"s": pltpu.SMEM, "v": pltpu.VMEM, "w": pltpu.VMEM, "h": pltpu.HBM, "r": pltpu.HBM}
    held = [a for a, k in zip(args, kinds) if k == "h"]
    sent = [o for o, k in zip(out, out_kinds) if k == "h"]

    def kernel(*refs):
        ins, outs = refs[: len(args)], refs[len(args) : len(args) + len(out)]
        rest = list(refs[len(args) + len(out) :])
        own, rest = rest[: len(scratch)], rest[len(scratch) :]
        sems = rest.pop()
        copies, given, back, straight = [], [], [], []
        for r, k in zip(ins, kinds):
            if k == "h":
                v = rest.pop(0)
                copies.append(pltpu.make_async_copy(r, v, sems.at[len(copies)]))
                given.append(v)
            elif k != "r":
                given.append(r)
        for r, k in zip(outs, out_kinds):
            if k == "h":
                v = rest.pop(0)
                back.append(pltpu.make_async_copy(v, r, sems.at[len(copies) + len(back)]))
                given.append(v)
            elif k != "r":
                given.append(r)
        for i, first, rows, o, to in direct:
            src, dst = ins[i], outs[o]
            if rows:
                at = first(*position()) if callable(first) else first
                at = pl.multiple_of(at, 16) if callable(first) else at
                src, dst = src.at[pl.ds(at, rows)], dst.at[pl.ds(to, rows)]
            sem = sems.at[len(copies) + len(back) + len(straight)]
            straight.append(pltpu.make_async_copy(src, dst, sem))
        for c in copies + straight:
            c.start()

        def ready(*which):
            for i in which or range(len(copies)):
                copies[i].wait()

        ready.rest = straight
        body(ready, *given, *own)
        for c in back:
            c.start()
        for c in back + straight:
            c.wait()

    buffers = [pltpu.VMEM(a.shape, a.dtype) for a in held + sent]
    return pl.pallas_call(
        kernel,
        out_shape=[
            (pltpu.HBM if k == "h" else pltpu.VMEM)(o.shape, o.dtype)
            for o, k in zip(out, out_kinds)
        ],
        in_specs=[pl.BlockSpec(memory_space=spaces[k]) for k in kinds],
        out_specs=[
            pl.BlockSpec(memory_space=pltpu.HBM if k == "h" else pltpu.VMEM) for k in out_kinds
        ],
        scratch_shapes=list(scratch) + buffers + [pltpu.SemaphoreType.DMA((24,))],
        compiler_params=pltpu.CompilerParams(vmem_limit_bytes=VMEM_LIMIT),
        cost_estimate=pl.CostEstimate(
            flops=int(micros * 1e12), bytes_accessed=int(micros * 3.5e6), transcendentals=0
        ),
    )(
        *[
            pltpu.with_memory_space_constraint(a, spaces[k]) if k in "whr" else a
            for a, k in zip(args, kinds)
        ]
    )


def shape(rows, cols, dtype=BF16):
    return jax.ShapeDtypeStruct((rows, cols), dtype)


def local(
    points,
    basis,
    transfer,
    top_transfer,
    coupling,
    far_index,
    far_count,
    top_coupling,
    top_index,
    top_count,
    near_block,
    near_index,
    near_count,
):
    devices = 512

    def like(*arrays):
        return [jax.ShapeDtypeStruct(a.shape, a.dtype) for a in arrays]

    root_msg, stack = call(
        up_kernel,
        [shape(512, 128), shape(1024, 128)],
        "hh",
        [],
        "hhh",
        (points, basis, transfer),
        COST[0],
    )
    plane_roots = lax.all_to_all(root_msg, PLANE, 0, 0, tiled=True)

    ex, chain, nested, rows, tops = call(
        exchange_kernel,
        [shape(512, 128), shape(128, 1152), shape(RANK, LPD * LEAF), shape(288, 1024)]
        + like(top_coupling),
        "hhhqr",
        [pltpu.VMEM((176, 1024), F32)],
        "hhhhrr",
        (stack, points, transfer, basis, top_transfer, top_coupling),
        COST[1],
        direct=[
            (4, 0, 128, 3, 0),
            (4, lambda y, low: 128 + (y * 64 + low) // 4 // 16 * 16, 16, 3, 240),
            (4, lambda y, low: 256 + (y * 64 + low) // 2 // 16 * 16, 16, 3, 256),
            (4, lambda y, low: 512 + (y * 64 + low) // 16 * 16, 16, 3, 272),
            (4, lambda y, low: 512 + 64 * y, 64, 3, 176),
            (4, lambda y, low: 256 + 32 * y, 32, 3, 144),
            (4, lambda y, low: 128 + 16 * y, 16, 3, 128),
            (5, 0, 0, 4, 0),
        ],
    )
    before = lax.ppermute(ex, ALL, [(i, i + 1) for i in range(devices - 1)])
    after = lax.ppermute(ex, ALL, [(i + 1, i) for i in range(devices - 1)])

    msg, own, first_rows = call(
        plane_kernel,
        [shape(8 * MSG, 128), shape(896, 128), shape(16, 1024)],
        "hvr",
        [pltpu.VMEM((128, 1024), F32)],
        "sswvvr",
        (top_index, top_count, plane_roots, rows, tops, top_transfer),
        COST[2],
        direct=[(5, 0, 16, 2, 0)],
    )
    planes = lax.all_to_all(msg, "y", 0, 0, tiled=True)
    (z_msg,) = call(
        top_kernel,
        [shape(1024, 128)],
        "h",
        [pltpu.VMEM((NODES * 16, 128), F32)],
        "wvv",
        (planes, own, first_rows),
        COST[3],
    )
    z_all = lax.all_to_all(z_msg, PLANE, 0, 0, tiled=True)
    rest, held_chain, held_nested = call(
        side_kernel,
        [shape(VEC, LPD * LEAF, F32)] + like(chain, nested),
        "vrr",
        [
            pltpu.VMEM((3072, 128), F32),
            pltpu.VMEM((1024, 1024), BF16),
            pltpu.VMEM((3104, 128), BF16),
            pltpu.VMEM((512, 256), BF16),
        ],
        "sssswhwhhhhhrr",
        (
            far_index,
            far_count,
            near_index,
            near_count,
            before,
            stack,
            after,
            points,
            coupling,
            transfer,
            basis,
            near_block,
            chain,
            nested,
        ),
        COST[4],
        direct=[(12, 0, 0, 1, 0), (13, 0, 0, 2, 0)],
    )
    (result,) = call(
        down_kernel,
        [shape(VEC, LPD * LEAF)],
        "h",
        [],
        "wvvv",
        (z_all, held_chain, held_nested, rest),
        COST[6],
    )
    return result


def solution(mesh):
    grid = Mesh(mesh.devices.reshape(8, 8, 2, 4), ALL)
    one, two, three = P(ALL), P(ALL, None), P(ALL, None, None)
    wide = P(None, ALL)
    placed = (wide, wide, two, P(), three, two, one, three, two, one, three, two, one)
    return jax.shard_map(local, mesh=grid, in_specs=placed, out_specs=wide, check_vma=False)
```
